128 devices in a mesh: blk: 16 (over y_lo, z, core), col: 8 (over x, y_hi).
Axes of the slice: x: 4, y: 4 (y_hi: 2, y_lo: 2; y = y_hi * 2 + y_lo), z: 4, core: 2. Of those that a mesh axis runs over, the one named last changes fastest.
Arguments:
- coords: bfloat16 [24576, 900], P(('blk', 'col')), may hold values from -30 to 30
- basis: bfloat16 [16, 24576], P(None, ('blk', 'col')), may hold values from -6 to 6
- pairs: int32 [16, 16], replicated, may hold values from 0 to 1, as said below
Outputs:
- diffused: float32 [16, 24576], P(None, ('blk', 'col'))
- density: float32 [24576], P(('blk', 'col'))
The draws below stay inside these ranges and needn't reach their ends.
Inputs may be any that keep to these rules, and one draw needn't show every extreme that they name: pairs is symmetric with ones on its diagonal; block 0 is a neighbour of every block.
All inputs are finite; a program needn't handle non-finite values.
Results may differ from the reference program's by a relative error of at most 0.0065.
Values may be sent and summed in bfloat16 or wider, within the bound.
No kernel may reach another device: no remote copies, remote signals or barrier semaphores. Data moves between devices by JAX's collectives and lax.ppermute only.
A program may use at most 64 MiB of HBM per device.

```python
import math
import jax
import jax.numpy as jnp
from jax import lax

D = 900
BASIS = 16
FRAMES = 24576
N_BLK = 16


def draw_coords(key, part):
    key = jax.random.fold_in(key, 11)
    key_scale, key_center, key_offset, key_jitter, key_embed, key_noise, key_state = jax.random.split(key, 7)
    clusters = FRAMES // 16
    states = 64
    spread = jnp.exp(jax.random.uniform(key_scale, (clusters, 1), jnp.float32, math.log(0.6), math.log(1.3)))
    state_ids = jax.random.randint(key_state, (clusters,), 0, states)
    centers = 0.74 * jax.random.normal(key_center, (states, D), jnp.float32)
    offsets = 0.3 * jax.random.normal(key_offset, (clusters, D), jnp.float32)
    jitter = 0.15 * jax.random.normal(key_jitter, (FRAMES, D), jnp.float32)
    noise_part = 0.3 * jax.random.normal(key_noise, (FRAMES, D), jnp.float32)
    embedding = jax.random.normal(key_embed, (D,), jnp.float32)
    cluster_place = spread * (centers[state_ids] + offsets)
    frame_ids = jnp.arange(FRAMES, dtype=jnp.int32)
    cluster_ids = frame_ids // 16
    location = cluster_place[cluster_ids] + jitter
    sampled = embedding[None, :] * location + noise_part
    return jnp.clip(sampled, -30.0, 30.0).astype(jnp.bfloat16)


def draw_pairs(key, part):
    key = jax.random.fold_in(key, 5)
    key_pair, key_level = jax.random.split(key, 2)
    scores = jax.random.randint(key_pair, (N_BLK, N_BLK), 0, 100)
    scores = jnp.maximum(scores, scores.T)
    levels = jax.random.randint(key_level, (N_BLK,), 0, 50)
    levels = jnp.where(jnp.arange(N_BLK) == 0, 100, levels)
    linked = scores < levels[:, None] + levels[None, :]
    linked = linked | (jnp.arange(N_BLK)[:, None] == jnp.arange(N_BLK)[None, :])
    return linked.astype(jnp.int32)


def steps_of(own_key, shape, pieces, least, largest):
    def one(position, shards_of):
        draws = jax.random.uniform(jax.random.fold_in(jax.random.fold_in(own_key, 6), position), (shards_of,), jnp.float32, least / len(pieces), largest / len(pieces))
        return jnp.repeat(jnp.exp(draws), shape[position] // shards_of).reshape((-1,) + (1,) * (len(shape) - position - 1))

    gain = one(*pieces[0])
    for cut in pieces[1:]:
        gain = gain * one(*cut)
    return gain


def bell_draw(stream_key, dims, deviation, most, cuts=(), held_as=jnp.bfloat16):
    factor_of = steps_of(stream_key, dims, cuts, -0.22, 0.18) if cuts else 1.0
    values = jax.random.normal(stream_key, dims, jnp.float32) * deviation * factor_of
    return jnp.minimum(jnp.maximum(values, -most), most).astype(held_as)


def setup_inputs(seed: int = 0) -> dict:
    key_list = jax.random.split(jax.random.key(seed), 4)
    coords = draw_coords(jax.random.fold_in(key_list[3], 71), 0)
    basis = bell_draw(key_list[1], (BASIS, FRAMES), 1.0, 6.0, ((1, 128),))
    pairs = draw_pairs(jax.random.fold_in(key_list[3], 71), 0)
    return dict(coords=coords, basis=basis, pairs=pairs)


def reference(coords, basis, pairs):
    frames = coords.shape[0]
    block_rows = frames // N_BLK
    values = coords.astype(jnp.float32)
    squares = jnp.sum(values * values, axis=1)
    owner = jnp.arange(frames, dtype=jnp.int32) // block_rows
    width = 0.25 * D

    def kernel_rows(block):
        start = (block * block_rows).astype(jnp.int32)
        local = lax.dynamic_slice_in_dim(values, start, block_rows, 0)
        local_sq = lax.dynamic_slice_in_dim(squares, start, block_rows, 0)
        gram = jnp.dot(local, values.T, precision=lax.Precision.HIGHEST)
        dist = local_sq[:, None] + squares[None, :] - 2.0 * gram
        neighbours = lax.dynamic_index_in_dim(pairs, block, 0, keepdims=False)[owner]
        return (neighbours.astype(jnp.float32)[None, :] * jnp.exp(-jnp.maximum(dist, 0.0) / width)).astype(jnp.bfloat16)

    blocks = jnp.arange(N_BLK, dtype=jnp.int32)
    density = lax.map(lambda b: jnp.sum(kernel_rows(b).astype(jnp.float32), axis=1), blocks).reshape(frames)
    inverse_f = 1.0 / density
    scaled = (basis.astype(jnp.float32) * inverse_f[None, :]).astype(jnp.bfloat16)
    inverse = inverse_f.astype(jnp.bfloat16)

    def second(block):
        kern = kernel_rows(block)
        numer = jnp.dot(scaled, kern.T, preferred_element_type=jnp.float32)
        denom = jnp.dot(kern, inverse, preferred_element_type=jnp.float32)
        return numer / denom[None, :]

    result = lax.map(second, blocks)
    return (jnp.transpose(result, (1, 0, 2)).reshape(BASIS, frames), density)
```

```python
import functools
import math

import jax
import jax.numpy as jnp
from jax import lax
from jax.experimental import pallas as pl
from jax.experimental.pallas import tpu as pltpu
from jax.sharding import Mesh, PartitionSpec as P

D = 900
LANES = 1024
SUB = 192
HALF = 96
AXES = ("ylo", "z", "core", "x", "yhi")
SIZES = (2, 4, 2, 4, 2)
SCALE = 2.0 * math.log2(math.e) / (0.25 * D)
NEG = -1e30


def fetch(array, **delta):
    pairs = []
    for dst in range(math.prod(SIZES)):
        rest, coords = dst, []
        for size in reversed(SIZES):
            coords.append(rest % size)
            rest //= size
        coords.reverse()
        src = 0
        for axis, size, at in zip(AXES, SIZES, coords):
            src = src * size + (at + delta.get(axis, 0)) % size
        pairs.append((src, dst))
    return lax.ppermute(array, AXES, pairs)


def kernel_tile(pairs_ref, *refs):
    n_in = 24
    ins, (kern_ref, dens_ref, basis_ref, rows, cols, sems) = refs[:n_in], refs[n_in:]
    step = pl.program_id(0)
    (r00, r10, r30, r01, r11, r31, fx1, fx3) = ins[:8]
    col_in = (ins[8:16], ins[16:24])
    row_copies, col_copies = [], [[], [], [], []]
    count = [0]

    def copy(src, src_at, dst, dst_at, n):
        k = count[0]
        count[0] += 1
        return pltpu.make_async_copy(
            src.at[pl.ds(src_at, n)], dst.at[pl.ds(dst_at, n)], sems.at[k]
        )

    for at, ref in ((0, r00), (1, r10), (3, r30), (4, r01), (5, r11), (7, r31)):
        row_copies.append(copy(ref, 0, rows, at * SUB, SUB))
    for k, at in ((0, 2), (1, 6)):
        row_copies.append(copy(fx1, k * HALF, rows, at * SUB, HALF))
        row_copies.append(copy(fx3, k * HALF, rows, at * SUB + HALF, HALF))
    for dc in range(2):
        c00, c01, c03, c10, c11, c13, fz1, fz3 = col_in[dc]
        for p, ref in ((0, c00), (1, c01), (3, c03), (4, c10), (5, c11), (7, c13)):
            col_copies[p // 2].append(copy(ref, 0, cols, p * 384 + dc * 128, 128))
            col_copies[p // 2].append(copy(ref, 128, cols, p * 384 + 256 + dc * 64, 64))
        for k, p in ((0, 2), (1, 6)):
            col_copies[p // 2].append(copy(fz1, k * HALF, cols, p * 384 + dc * 128, HALF))
            col_copies[p // 2].append(copy(fz3, k * HALF, cols, p * 384 + dc * 128 + HALF, 32))
            col_copies[p // 2].append(
                copy(fz3, k * HALF + 32, cols, p * 384 + 256 + dc * 64, 64)
            )

    @pl.when(step == 0)
    def _():
        for c in row_copies:
            c.start()
        for group in col_copies:
            for c in group:
                c.start()
        for c in row_copies:
            c.wait()

    for s in range(4):

        @pl.when(step == s)
        def _(s=s):
            for c in col_copies[s]:
                c.wait()

    ylo, z, core = lax.axis_index("ylo"), lax.axis_index("z"), lax.axis_index("core")
    mine = (ylo * 4 + z) * 2 + core
    limits = []
    lane = lax.broadcasted_iota(jnp.int32, (1, 128), 1)
    for k in range(2):
        p = step * 2 + k
        dyl, dz = p // 4, p % 4
        pair = (lax.rem(ylo + dyl, 2) * 4 + lax.rem(z + dz, 4)) * 2
        a = jnp.where(pairs_ref[mine, pair + core] > 0, 0.0, NEG)
        b = jnp.where(pairs_ref[mine, pair + 1 - core] > 0, 0.0, NEG)
        limits += [
            jnp.full((1, 128), a, jnp.float32),
            jnp.full((1, 128), b, jnp.float32),
            jnp.where(lane < 64, a, b),
        ]
    for n in range(3):
        limit = jnp.concatenate(limits[2 * n : 2 * n + 2], axis=1)
        part = cols[pl.ds(pl.multiple_of(step * 768 + n * 256, 256), 256), :]
        basis_ref[:, n * 256 : (n + 1) * 256] = part[:, 896:].astype(jnp.float32).T[16:32].astype(
            jnp.bfloat16
        )
        total = jnp.zeros((1, 256), jnp.float32)
        for m in range(3):
            gram = lax.dot_general(
                rows[m * 512 : (m + 1) * 512, :],
                part,
                (((1,), (1,)), ((), ())),
                preferred_element_type=jnp.float32,
            )
            kern = jnp.exp2(jnp.minimum(gram * SCALE, limit)).astype(jnp.bfloat16)
            kern_ref[m * 512 : (m + 1) * 512, n * 256 : (n + 1) * 256] = kern
            total += jnp.sum(kern.astype(jnp.float32), axis=0, keepdims=True)
        dens_ref[0, 2 * n : 2 * n + 1, :] = total[:, :128]
        dens_ref[0, 2 * n + 1 : 2 * n + 2, :] = total[:, 128:]


def apply_tile(dens_ref, basis_ref, kern_ref, out_ref, scaled):
    @pl.when(pl.program_id(0) == 0)
    def _():
        for k in range(24):
            inverse = 1.0 / dens_ref[k : k + 1, :]
            at = slice(k * 128, (k + 1) * 128)
            scaled[:16, at] = (basis_ref[:, at].astype(jnp.float32) * inverse).astype(jnp.bfloat16)
            row = lax.broadcasted_iota(jnp.int32, (16, 128), 0)
            scaled[16:, at] = jnp.where(row == 0, inverse, 0.0).astype(jnp.bfloat16)

    both = lax.dot_general(
        scaled[...], kern_ref[...], (((1,), (1,)), ((), ())), preferred_element_type=jnp.float32
    )
    out_ref[0] = both[:24, :SUB]
    out_ref[1] = both[:24, SUB:]


def body(coords, basis, pairs):
    values = coords.astype(jnp.float32)
    sq = -0.5 * jnp.sum(values * values, axis=1, keepdims=True)
    high = lax.reduce_precision(sq, 8, 7)
    mid = lax.reduce_precision(sq - high, 8, 7)
    low = lax.reduce_precision(sq - high - mid, 8, 7)
    parts = jnp.concatenate([high, mid, low], axis=1).astype(jnp.bfloat16)
    ones = jnp.ones((SUB, 3), jnp.bfloat16)
    zeros = lambda n: jnp.zeros((SUB, n), jnp.bfloat16)
    v = jnp.concatenate([coords, parts, ones, zeros(LANES - 906)], axis=1)
    w = jnp.concatenate([coords, ones, parts, zeros(6), basis.T, zeros(LANES - 928)], axis=1)

    r01 = fetch(v, yhi=1)
    c10 = fetch(w, ylo=1)
    r10, r30 = fetch(v, x=1), fetch(v, x=-1)
    c01, c03 = fetch(w, z=1), fetch(w, z=-1)
    r11, r31 = fetch(r01, x=1), fetch(r01, x=-1)
    c11, c13 = fetch(c10, z=1), fetch(c10, z=-1)
    fx1 = fetch(jnp.concatenate([r10[:HALF], r11[:HALF]]), x=1)
    fx3 = fetch(jnp.concatenate([r30[HALF:], r31[HALF:]]), x=-1)
    fz1 = fetch(jnp.concatenate([c01[:HALF], c11[:HALF]]), z=1)
    fz3 = fetch(jnp.concatenate([c03[HALF:], c13[HALF:]]), z=-1)
    col_in = (w, c01, c03, c10, c11, c13, fz1, fz3)
    other = tuple(fetch(a, core=1) for a in col_in)

    any_spec = pl.BlockSpec(memory_space=pl.ANY)
    kern, dens, basis_cols = pl.pallas_call(
        kernel_tile,
        grid=(4,),
        in_specs=[pl.BlockSpec(memory_space=pltpu.SMEM)] + [any_spec] * 24,
        out_specs=[
            pl.BlockSpec((1536, 768), lambda i: (0, i)),
            pl.BlockSpec((1, 6, 128), lambda i: (i, 0, 0)),
            pl.BlockSpec((16, 768), lambda i: (0, i)),
        ],
        out_shape=[
            jax.ShapeDtypeStruct((1536, 3072), jnp.bfloat16),
            jax.ShapeDtypeStruct((4, 6, 128), jnp.float32),
            jax.ShapeDtypeStruct((16, 3072), jnp.bfloat16),
        ],
        scratch_shapes=[
            pltpu.VMEM((1536, LANES), jnp.bfloat16),
            pltpu.VMEM((3072, LANES), jnp.bfloat16),
            pltpu.SemaphoreType.DMA((46,)),
        ],
        compiler_params=pltpu.CompilerParams(vmem_limit_bytes=40 * 2**20),
        name="kernel_tile",
    )(pairs, r00 := v, r10, r30, r01, r11, r31, fx1, fx3, *col_in, *other)

    t = dens.reshape(2, 4, 3, 128)

    def other_core(a):
        return jnp.concatenate([a[:, :, 1:2], a[:, :, 0:1], jnp.roll(a[:, :, 2:], 64, axis=3)], axis=2)

    t = t + other_core(fetch(t, core=1))
    t = t + jnp.roll(fetch(t, ylo=1), 1, axis=0)
    t = (
        t
        + jnp.roll(fetch(t, z=1), 1, axis=1)
        + jnp.roll(fetch(t, z=-1), -1, axis=1)
        + jnp.roll(fetch(t, z=2), 2, axis=1)
    )
    density = jnp.concatenate([t[0, 0, 0], t[0, 0, 2, :64]])

    both = pl.pallas_call(
        apply_tile,
        grid=(4,),
        in_specs=[
            pl.BlockSpec((24, 128), lambda i: (0, 0)),
            pl.BlockSpec((16, 3072), lambda i: (0, 0)),
            pl.BlockSpec((384, 3072), lambda i: (i, 0)),
        ],
        out_specs=pl.BlockSpec((2, 24, SUB), lambda i: (i, 0, 0)),
        out_shape=jax.ShapeDtypeStruct((8, 24, SUB), jnp.float32),
        scratch_shapes=[pltpu.VMEM((32, 3072), jnp.bfloat16)],
        compiler_params=pltpu.CompilerParams(vmem_limit_bytes=40 * 2**20),
        name="apply_tile",
    )(t.reshape(24, 128), basis_cols, kern)

    own = both[:4] + fetch(both[4:], yhi=1)
    own = own[0] + fetch(own[1], x=-1) + fetch(own[3], x=1) + fetch(own[2], x=2)
    return own[:16] / own[16:17], density


def solution(mesh):
    physical = Mesh(mesh.devices.reshape(SIZES), AXES)
    return jax.shard_map(
        body,
        mesh=physical,
        in_specs=(P(AXES, None), P(None, AXES), P()),
        out_specs=(P(None, AXES), P(AXES)),
        check_vma=False,
    )
```

```python
import functools
import math

import jax
import jax.numpy as jnp
from jax import lax
from jax.experimental import pallas as pl
from jax.experimental.pallas import tpu as pltpu
from jax.sharding import Mesh, PartitionSpec as P

D = 900
LANES = 1024
SUB = 192
HALF = 96
CHUNK = 2 * SUB
WIDE = 256
AXES = ("ylo", "z", "core", "x", "yhi")
SIZES = (2, 4, 2, 4, 2)
SCALE = 2.0 * math.log2(math.e) / (0.25 * D)
NEG = -1e30
ROW_ORDER = ((0, 0), (1, 0), (3, 0), (0, 1), (1, 1), (3, 1), (2, 0), (2, 1))
EARLY = tuple((0, dz, dc) for dc in (0, 1) for dz in (0, 1, 3))
LATE = tuple(tuple((dyl, dz, dc) for dyl, dz in ((0, 2), (1, 0), (1, 1), (1, 3), (1, 2))) for dc in (0, 1))
LATE_PAD = 64
VMEM = pl.BlockSpec(memory_space=pltpu.VMEM)
SMEM = pl.BlockSpec(memory_space=pltpu.SMEM)


def params(mib):
    return pltpu.CompilerParams(vmem_limit_bytes=mib * 2**20)


def fetch(array, **delta):
    pairs = []
    for dst in range(math.prod(SIZES)):
        rest, coords = dst, []
        for size in reversed(SIZES):
            coords.append(rest % size)
            rest //= size
        coords.reverse()
        src = 0
        for axis, size, at in zip(AXES, SIZES, coords):
            src = src * size + (at + delta.get(axis, 0)) % size
        pairs.append((src, dst))
    return lax.ppermute(array, AXES, pairs)


def together(*arrays):
    return lax.optimization_barrier(arrays)


def prepare(coords_ref, basis_ref, v_ref, w_ref):
    values = coords_ref[...].astype(jnp.float32)
    sq = -0.5 * jnp.sum(values * values, axis=1, keepdims=True)
    high = sq.astype(jnp.bfloat16).astype(jnp.float32)
    mid = (sq - high).astype(jnp.bfloat16).astype(jnp.float32)
    low = (sq - high - mid).astype(jnp.bfloat16).astype(jnp.float32)
    lane = lax.broadcasted_iota(jnp.int32, (SUB, 128), 1)
    tail = jnp.concatenate([values[:, 896:], jnp.zeros((SUB, 124), jnp.float32)], axis=1)
    basis = jnp.concatenate(
        [jnp.zeros((16, SUB)), basis_ref[...].astype(jnp.float32), jnp.zeros((96, SUB))], axis=0
    ).T

    def fill(first, ones_at, rest):
        out = jnp.where(lane == first, high, rest)
        out = jnp.where(lane == first + 1, mid, out)
        out = jnp.where(lane == first + 2, low, out)
        return jnp.where((lane >= ones_at) & (lane < ones_at + 3), 1.0, out).astype(jnp.bfloat16)

    v_ref[:, :896] = coords_ref[:, :896]
    w_ref[:, :896] = coords_ref[:, :896]
    v_ref[:, 896:] = fill(4, 7, tail)
    w_ref[:, 896:] = fill(7, 4, tail + basis)


def place(shard):
    dyl, dz, dc = shard
    ylo = lax.rem(lax.axis_index("ylo") + dyl, 2)
    z = lax.rem(lax.axis_index("z") + dz, 4)
    core = lax.rem(lax.axis_index("core") + dc, 2)
    return (ylo * 4 + z) * 2 + core


def tile_kernel(jobs, shards, n_rows, n_old, known, pairs_ref, *refs):
    n_cols = len(shards)
    rows, cols, refs = refs[:n_rows], refs[n_rows : n_rows + n_cols], refs[n_rows + n_cols :]
    old, refs = refs[:n_old], refs[n_old:]
    outs, dens_ref, basis_refs = refs[: len(jobs)], refs[len(jobs)], refs[len(jobs) + 1 :]
    mine = place((0, 0, 0))
    if old:
        dens_ref[...] = old[0][...]
    seen = set()
    for row_at, col_at, out in jobs:
        width = cols[col_at].shape[0]
        lane = lax.broadcasted_iota(jnp.int32, (1, width), 1)
        limit = jnp.full((1, width), NEG, jnp.float32)
        for k, shard in enumerate(shards[col_at]):
            block = place(shard)
            here = (lane >= k * SUB) & (lane < (k + 1) * SUB)
            limit = jnp.where(here, jnp.where(pairs_ref[mine, block] > 0, 0.0, NEG), limit)
        totals = []
        for at in range(0, width, WIDE):
            ns = slice(at, min(at + WIDE, width))
            n = ns.stop - ns.start
            total = jnp.zeros((8, n), jnp.float32)
            for m in range(0, rows[row_at].shape[0], CHUNK):
                ms = slice(m, m + CHUNK)
                gram = lax.dot_general(
                    rows[row_at][ms, :],
                    cols[col_at][ns, :],
                    (((1,), (1,)), ((), ())),
                    preferred_element_type=jnp.float32,
                )
                kern = jnp.exp2(jnp.minimum(gram * SCALE, limit[:, ns])).astype(jnp.bfloat16)
                outs[out][ms, ns] = kern
                total += jnp.sum(kern.astype(jnp.float32).reshape(CHUNK // 8, 8, n), axis=0)
            totals.append(jnp.sum(total, axis=0, keepdims=True))
        totals = jnp.concatenate(totals, axis=1)
        fresh = col_at not in seen and col_at >= known
        for k, shard in enumerate(shards[col_at]):
            row = place(shard)
            part = totals[:, k * SUB : (k + 1) * SUB]
            if not fresh:
                part += dens_ref[pl.ds(row, 1), :]
            dens_ref[pl.ds(row, 1), :] = part
        if fresh:
            part = cols[col_at][:, 896:].astype(jnp.float32).T
            basis_refs[col_at - known][...] = part[16:32].astype(jnp.bfloat16)
        seen.add(col_at)


def tile_call(name, pairs, rows, cols, shards, jobs, old=()):
    known = 1 if old and len(cols) > 1 else 0
    shapes = [(rows[r].shape[0], cols[c].shape[0]) for r, c, _ in jobs]
    units = sum(a * b for a, b in shapes)
    return pl.pallas_call(
        functools.partial(tile_kernel, jobs, shards, len(rows), len(old), known),
        in_specs=[SMEM] + [VMEM] * (len(rows) + len(cols) + len(old)),
        out_specs=[VMEM] * (len(shapes) + 1 + len(cols) - known),
        out_shape=[jax.ShapeDtypeStruct(s, jnp.bfloat16) for s in shapes]
        + [jax.ShapeDtypeStruct((16, SUB), jnp.float32)]
        + [jax.ShapeDtypeStruct((16, c.shape[0]), jnp.bfloat16) for c in cols[known:]],
        compiler_params=params(12),
        cost_estimate=pl.CostEstimate(
            flops=units * LANES * 2, bytes_accessed=units, transcendentals=units
        ),
        name=name,
    )(pairs, *rows, *cols, *old)


def apply_kernel(t0, t1, t2, t3, be, bo, bt, kae, kbe, kao, kbo, kat, kbt, here_ref, there_ref, density_ref, inv, se, so, st):
    row = place((0, 0, 0))
    total = t0[...] + t1[...] + t2[...] + t3[...]
    inv[...] = total
    density_ref[...] = inv[pl.ds(row, 1), :]
    inv[...] = 1.0 / total
    for shards, basis, scaled in ((EARLY, be, se), (LATE[0], bo, so), (LATE[1], bt, st)):
        parts = [inv[pl.ds(place(s), 1), :] for s in shards]
        if scaled.shape[1] > len(shards) * SUB:
            parts.append(jnp.zeros((1, scaled.shape[1] - len(shards) * SUB), jnp.float32))
        inverse = jnp.concatenate(parts, axis=1)
        first = lax.broadcasted_iota(jnp.int32, (16, scaled.shape[1]), 0) == 0
        scaled[:16, :] = (basis[...].astype(jnp.float32) * inverse).astype(jnp.bfloat16)
        scaled[16:, :] = jnp.where(first, inverse, 0.0).astype(jnp.bfloat16)
    for s in range(4):
        group = ((se, kae), (so, kao), (st, kat)) if s < 3 else ((se, kbe), (so, kbo), (st, kbt))
        ms = slice(s * CHUNK, (s + 1) * CHUNK) if s < 3 else slice(0, CHUNK)
        both = sum(
            lax.dot_general(
                scaled[...],
                kern[ms, :],
                (((1,), (1,)), ((), ())),
                preferred_element_type=jnp.float32,
            )
            for scaled, kern in group
        )
        for k in range(2):
            dx, dy = ROW_ORDER[2 * s + k]
            (there_ref if dy else here_ref)[dx] = both[:24, k * SUB : (k + 1) * SUB]


def finish(a_ref, b_ref, c_ref, d_ref, out_ref):
    total = a_ref[...] + b_ref[...] + c_ref[...] + d_ref[...]
    out_ref[...] = total[:16] / total[16:17]


def body(coords, basis, pairs):
    bf16 = lambda *s: jax.ShapeDtypeStruct(s, jnp.bfloat16)
    f32 = lambda *s: jax.ShapeDtypeStruct(s, jnp.float32)
    v, w = pl.pallas_call(
        prepare,
        in_specs=[VMEM] * 2,
        out_specs=[VMEM] * 2,
        out_shape=[bf16(SUB, LANES)] * 2,
        compiler_params=params(8),
        name="prepare",
    )(coords, basis)

    r01, r10, r30, c01, c03, w2 = together(
        fetch(v, yhi=1), fetch(v, x=1), fetch(v, x=-1), fetch(w, z=1), fetch(w, z=-1), w
    )
    r11, r31 = fetch(r01, x=1), fetch(r01, x=-1)
    c10, c02 = fetch(w2, ylo=1), fetch(w2, z=2)
    own_e = jnp.concatenate([w2, c01, c03])
    other_e = fetch(own_e, core=1)
    r11, r31, c10, c02, other_e = together(r11, r31, c10, c02, other_e)
    fx1 = fetch(jnp.concatenate([r10[:HALF], r11[:HALF]]), x=1)
    fx3 = fetch(jnp.concatenate([r30[HALF:], r31[HALF:]]), x=-1)
    c11, c13, c12 = fetch(c10, z=1), fetch(c10, z=-1), fetch(c02, ylo=1)
    rows_a = jnp.concatenate([v, r10, r30, r01, r11, r31])
    cols_e = jnp.concatenate([own_e, other_e])
    kae, dens, be = tile_call("tile_first", pairs, (rows_a,), (cols_e,), (EARLY,), ((0, 0, 0),))
    fx1, fx3, c11, c13, c12, dens = together(fx1, fx3, c11, c13, c12, dens)
    rows_b = jnp.concatenate([fx1[:HALF], fx3[:HALF], fx1[HALF:], fx3[HALF:]])
    own = jnp.concatenate([c02, c10, c11, c13, c12, jnp.zeros((LATE_PAD, LANES), jnp.bfloat16)])
    other = fetch(own, core=1)
    kao, kbo, kbe, dens, bo = tile_call(
        "tile_second",
        pairs,
        (rows_a, rows_b),
        (cols_e, own),
        (EARLY, LATE[0]),
        ((0, 1, 0), (1, 1, 1), (1, 0, 2)),
        (dens,),
    )
    kat, kbt, dens, bt = tile_call(
        "tile_third", pairs, (rows_a, rows_b), (other,), (LATE[1],), ((0, 0, 0), (1, 0, 1)), (dens,)
    )

    t = dens + fetch(dens, core=1)
    t = t + fetch(t, ylo=1)
    here, there, density = pl.pallas_call(
        apply_kernel,
        in_specs=[VMEM] * 13,
        out_specs=[VMEM] * 3,
        out_shape=[f32(4, 24, SUB), f32(4, 24, SUB), f32(1, SUB)],
        scratch_shapes=[pltpu.VMEM((16, SUB), jnp.float32)]
        + [pltpu.VMEM((32, b.shape[1]), jnp.bfloat16) for b in (be, bo, bt)],
        compiler_params=params(12),
        name="apply_tile",
    )(t, fetch(t, z=1), fetch(t, z=2), fetch(t, z=-1), be, bo, bt, kae, kbe, kao, kbo, kat, kbt)

    sums = here + fetch(there, yhi=1)
    diffused = pl.pallas_call(
        finish,
        in_specs=[VMEM] * 4,
        out_specs=VMEM,
        out_shape=f32(16, SUB),
        compiler_params=params(8),
        name="finish",
    )(sums[0], fetch(sums[1], x=-1), fetch(sums[3], x=1), fetch(sums[2], x=2))
    return diffused, density.reshape(SUB)


def solution(mesh):
    physical = Mesh(mesh.devices.reshape(SIZES), AXES)
    return jax.shard_map(
        body,
        mesh=physical,
        in_specs=(P(AXES, None), P(None, AXES), P()),
        out_specs=(P(None, AXES), P(AXES)),
        check_vma=False,
    )
```

```python
import functools
import math

import jax
import jax.numpy as jnp
from jax import lax
from jax.experimental import pallas as pl
from jax.experimental.pallas import tpu as pltpu
from jax.sharding import Mesh, PartitionSpec as P

D = 900
LANES = 1024
SUB = 192
CHUNK = 2 * SUB
WIDE = 256
AXES = ("ylo", "z", "core", "x", "yhi")
SIZES = (2, 4, 2, 4, 2)
SCALE = 2.0 * math.log2(math.e) / (0.25 * D)
NEG = -1e30
ROW_PAIR = dict(ylo=1)
COL_PAIR = dict(ylo=1, yhi=1)
CHIPS = ((0, 0), (1, 0), (3, 0), (0, 1), (2, 0), (1, 1), (3, 1), (2, 1))
ROWS = ((0, 1, 2, 3), (4, 5, 6), (7,))
PARTS = (
    tuple((chip, core) for chip in (0, 1, 2, 3) for core in (1, 0)),
    ((4, 1), (5, 1), (4, 0), (6, 0), (5, 0), (6, 1)),
    ((7, 1), (7, 0)),
)
ROW_COPIES = (
    tuple(tuple((k, core * SUB, k * SUB, SUB) for k in range(4)) for core in (0, 1)),
    (((0, 0, 0, SUB), (0, SUB, SUB, SUB), (2, SUB, CHUNK, SUB)),
     ((1, 0, 0, SUB), (2, 0, SUB, SUB), (1, SUB, CHUNK, SUB))),
    (((0, 0, 0, 128), (2, 0, 128, 64)), ((1, 0, 0, 128), (2, 64, 128, 64))),
)
COL_COPIES = (
    tuple((k, 0, k * CHUNK, CHUNK) for k in range(4)),
    tuple((k, 0, k * CHUNK, CHUNK) for k in range(3)),
    ((0, 0, 0, 128), (2, 0, 128, 64), (1, 0, SUB, 128), (2, 64, SUB + 128, 64)),
)
N_ROWS = tuple(len(r) * SUB for r in ROWS)
N_COLS = tuple(len(c) * SUB for c in PARTS)
ARRAYS = (4, 3, 3)
VMEM = pl.BlockSpec(memory_space=pltpu.VMEM)
SMEM = pl.BlockSpec(memory_space=pltpu.SMEM)


def params(mib):
    return pltpu.CompilerParams(vmem_limit_bytes=mib * 2**20)


def fetch(array, first, second=None):
    pairs = []
    for dst in range(math.prod(SIZES)):
        rest, coords = dst, []
        for size in reversed(SIZES):
            coords.append(rest % size)
            rest //= size
        coords.reverse()
        delta = second if second is not None and coords[2] else first
        src = 0
        for axis, size, at in zip(AXES, SIZES, coords):
            by = delta.get(axis, 0)
            src = src * size + (by(at) if callable(by) else (at + by) % size)
        pairs.append((src, dst))
    return lax.ppermute(array, AXES, pairs)


def along(array, by):
    return fetch(array, dict(x=by), dict(z=by))


def across(array):
    return fetch(array, ROW_PAIR, COL_PAIR)


def swap(array):
    return fetch(array, dict(core=1))


def together(*arrays):
    return lax.optimization_barrier(arrays)


def forms(ref, basis_ref):
    lane = lax.broadcasted_iota(jnp.int32, (SUB, 128), 1)
    values = ref[...].astype(jnp.float32)
    sq = -0.5 * jnp.sum(values * values, axis=1, keepdims=True)
    high = sq.astype(jnp.bfloat16).astype(jnp.float32)
    mid = (sq - high).astype(jnp.bfloat16).astype(jnp.float32)
    low = (sq - high - mid).astype(jnp.bfloat16).astype(jnp.float32)
    tail = jnp.concatenate([values[:, 896:], jnp.zeros((SUB, 124), jnp.float32)], axis=1)
    basis = basis_ref[...].astype(jnp.float32)
    basis = jnp.concatenate([jnp.zeros((16, SUB)), basis, jnp.zeros((96, SUB))], axis=0).T

    def fill(first, ones_at, rest):
        out = jnp.where(lane == first, high, rest)
        out = jnp.where(lane == first + 1, mid, out)
        out = jnp.where(lane == first + 2, low, out)
        return jnp.where((lane >= ones_at) & (lane < ones_at + 3), 1.0, out)

    row_form, col_form = fill(4, 7, tail), fill(7, 4, tail + basis)
    is_first = lax.axis_index("core") == 0
    moved = jnp.where(is_first, row_form, col_form).astype(jnp.bfloat16)
    return moved, jnp.where(is_first, col_form, row_form).astype(jnp.bfloat16)


def prepare(coords_ref, basis_ref, out_ref):
    out_ref[:SUB, :896] = coords_ref[:, :896]
    out_ref[SUB:, :896] = coords_ref[:, :896]
    out_ref[:SUB, 896:], out_ref[SUB:, 896:] = forms(coords_ref, basis_ref)


def prepare_other(own_ref, coords_ref, basis_ref, base_ref, swapped_ref):
    base_ref[:SUB], swapped_ref[SUB:] = own_ref[:SUB], own_ref[SUB:]
    base_ref[SUB:, :896] = coords_ref[:, :896]
    swapped_ref[:SUB, :896] = coords_ref[:, :896]
    base_ref[SUB:, 896:], swapped_ref[:SUB, 896:] = forms(coords_ref, basis_ref)


def block_of(chip, core):
    dz, dyl = CHIPS[chip]
    ylo = lax.rem(lax.axis_index("ylo") + dyl, 2)
    return (ylo * 4 + lax.rem(lax.axis_index("z") + dz, 4)) * 2 + core


def tile_kernel(part, jobs, row_ids, col_ids, fresh, pairs_ref, *refs):
    n_new = 0 if part is None else ARRAYS[part]
    moved, swapped, refs = refs[:n_new], refs[n_new : 2 * n_new], refs[2 * n_new :]
    rows = dict(zip(row_ids, refs))
    cols = dict(zip(col_ids, refs[len(row_ids) :]))
    refs = refs[len(row_ids) + len(col_ids) :]
    old, refs = (None, refs) if part == 0 else (refs[0], refs[1:])
    outs, dens_ref, refs = refs[: len(jobs)], refs[len(jobs)], refs[len(jobs) + 1 :]
    core = lax.axis_index("core")
    if part is not None:
        basis_ref, rows[part], cols[part], sems = refs
        for is_first in (True, False):

            @pl.when((core == 0) == is_first)
            def _(is_first=is_first):
                row_from, col_from = (moved, swapped) if is_first else (swapped, moved)
                plan = [(row_from, rows[part], c) for c in ROW_COPIES[part][0 if is_first else 1]]
                plan += [(col_from, cols[part], c) for c in COL_COPIES[part]]
                copies = [
                    pltpu.make_async_copy(
                        src[k].at[pl.ds(at, n)], dst.at[pl.ds(to, n)], sems.at[sem]
                    )
                    for sem, (src, dst, (k, at, to, n)) in enumerate(plan)
                ]
                for c in copies:
                    c.start()
                for c in copies:
                    c.wait()

    if old is not None:
        dens_ref[...] = old[...]
    started = set()
    for out, (r, c) in enumerate(jobs):
        width = N_COLS[c]
        lane = lax.broadcasted_iota(jnp.int32, (1, width), 1)
        limits = {}
        for pair in sorted({CHIPS[k][1] for k in ROWS[r]}):
            limit = jnp.zeros((1, width), jnp.float32)
            for k, (chip, of) in enumerate(PARTS[c]):
                here = (lane >= k * SUB) & (lane < (k + 1) * SUB)
                live = pairs_ref[block_of(3 * pair, core), block_of(chip, of)] > 0
                limit = jnp.where(here, jnp.where(live, 0.0, NEG), limit)
            limits[pair] = limit
        totals = []
        chunk = CHUNK if r == 0 else N_ROWS[r]
        for at in range(0, width, WIDE):
            ns = slice(at, min(at + WIDE, width))
            n = ns.stop - ns.start
            total = jnp.zeros((8, n), jnp.float32)
            for m in range(0, N_ROWS[r], chunk):
                gram = lax.dot_general(
                    rows[r][m : m + chunk, :],
                    cols[c][ns, :],
                    (((1,), (1,)), ((), ())),
                    preferred_element_type=jnp.float32,
                )
                for k in range(chunk // SUB):
                    limit = limits[CHIPS[ROWS[r][m // SUB + k]][1]][:, ns]
                    kern = jnp.minimum(gram[k * SUB : (k + 1) * SUB] * SCALE, limit)
                    kern = jnp.exp2(kern).astype(jnp.bfloat16)
                    outs[out][m + k * SUB : m + (k + 1) * SUB, ns] = kern
                    total += jnp.sum(kern.astype(jnp.float32).reshape(SUB // 8, 8, n), axis=0)
            totals.append(jnp.sum(total, axis=0, keepdims=True))
        totals = jnp.concatenate(totals, axis=1)
        first = c in fresh and c not in started
        started.add(c)
        for k, (chip, of) in enumerate(PARTS[c]):
            row = pl.ds(block_of(chip, of), 1)
            total = totals[:, k * SUB : (k + 1) * SUB]
            dens_ref[row, :] = total if first else total + dens_ref[row, :]
    if part is not None:
        tail = cols[part][:, 896:].astype(jnp.float32).T
        basis_ref[...] = tail[16:32].astype(jnp.bfloat16)


def tile_call(pairs, jobs, rows, cols, old=None, part=None, moved=(), swapped=(), fresh=()):
    shapes = [(N_ROWS[r], N_COLS[c]) for r, c in jobs]
    units = sum(a * b for a, b in shapes)
    bf16 = lambda *s: jax.ShapeDtypeStruct(s, jnp.bfloat16)
    row_ids, col_ids = tuple({r: 0 for r, _ in jobs}), tuple({c: 0 for _, c in jobs})
    row_ids = tuple(r for r in row_ids if r != part)
    col_ids = tuple(c for c in col_ids if c != part)
    out_shape = [bf16(*s) for s in shapes] + [jax.ShapeDtypeStruct((16, SUB), jnp.float32)]
    if part is not None:
        out_shape += [bf16(16, N_COLS[part]), bf16(N_ROWS[part], LANES), bf16(N_COLS[part], LANES)]
    operands = (
        *moved,
        *swapped,
        *[rows[r] for r in row_ids],
        *[cols[c] for c in col_ids],
        *(() if old is None else (old,)),
    )
    result = pl.pallas_call(
        functools.partial(tile_kernel, part, jobs, row_ids, col_ids, fresh),
        in_specs=[SMEM] + [VMEM] * len(operands),
        out_specs=[VMEM] * len(out_shape),
        out_shape=out_shape,
        scratch_shapes=[] if part is None else [pltpu.SemaphoreType.DMA((8,))],
        compiler_params=params(12),
        cost_estimate=pl.CostEstimate(flops=units, bytes_accessed=units, transcendentals=0),
        name="tile_part",
    )(pairs, *operands)
    n = len(jobs)
    kern, dens = dict(zip(jobs, result[:n])), result[n]
    if part is None:
        return kern, dens
    rows[part], cols[part] = result[n + 2 :]
    return kern, dens, result[n + 1]


def scale_kernel(keys, t0, t1, b0, b1, b2, *refs):
    kern, refs = dict(zip(keys, refs)), refs[len(keys) :]
    there_ref, density_ref, s0, s1, s2, inv = refs
    total = t0[...] + t1[...]
    inv[...] = total
    density_ref[...] = inv[pl.ds(block_of(0, lax.axis_index("core")), 1), :]
    inv[...] = 1.0 / total
    for part, basis, scaled in zip(PARTS, (b0, b1, b2), (s0, s1, s2)):
        inverse = jnp.concatenate([inv[pl.ds(block_of(*s), 1), :] for s in part], axis=1)
        first = lax.broadcasted_iota(jnp.int32, (16, inverse.shape[1]), 0) == 0
        scaled[:16, :] = (basis[...].astype(jnp.float32) * inverse).astype(jnp.bfloat16)
        scaled[16:, :] = jnp.where(first, inverse, 0.0).astype(jnp.bfloat16)
    row_sums(1, (s0, s1, s2), kern, there_ref)


def here_kernel(keys, s0, s1, s2, *refs):
    row_sums(0, (s0, s1, s2), dict(zip(keys, refs)), refs[len(keys)])


def row_sums(pair, scaled, kern, out_ref):
    for r in range(3):
        at = [k for k, chip in enumerate(ROWS[r]) if CHIPS[chip][1] == pair]
        if not at:
            continue
        ms = slice(at[0] * SUB, (at[-1] + 1) * SUB)
        both = sum(
            lax.dot_general(
                s[...],
                kern[r, c][ms, :],
                (((1,), (1,)), ((), ())),
                preferred_element_type=jnp.float32,
            )
            for c, s in enumerate(scaled)
        )
        for k in at:
            part = both[:24, (k - at[0]) * SUB : (k - at[0] + 1) * SUB]
            out_ref[CHIPS[ROWS[r][k]][0]] = part


def finish(a_ref, b_ref, c_ref, d_ref, out_ref):
    total = a_ref[...] + b_ref[...] + c_ref[...] + d_ref[...]
    out_ref[...] = total[:16] / total[16:17]


def body(coords, basis, pairs):
    f32 = lambda *s: jax.ShapeDtypeStruct(s, jnp.float32)
    form = lambda *s: jax.ShapeDtypeStruct((CHUNK, LANES), jnp.bfloat16)
    own = pl.pallas_call(
        prepare,
        in_specs=[VMEM] * 2,
        out_specs=VMEM,
        out_shape=form(),
        compiler_params=params(8),
        name="prepare",
    )(coords, basis)
    base, base_swapped = pl.pallas_call(
        prepare_other,
        in_specs=[VMEM] * 3,
        out_specs=[VMEM] * 2,
        out_shape=[form(), form()],
        compiler_params=params(8),
        name="prepare_other",
    )(own, swap(coords), swap(basis))
    join = lambda *arrays: jnp.concatenate(arrays)
    cut = lambda a: [a[k * CHUNK : (k + 1) * CHUNK] for k in range(a.shape[0] // CHUNK)]

    up, down, over = together(along(base, 1), along(base, -1), across(base))
    far_up = along(join(up[:SUB], over[:SUB]), 1)
    far_down = along(join(down[SUB:], over[SUB:]), -1)
    sides = across(join(up[SUB:], down[:SUB]))
    swapped = swap(join(up, down, over))
    rows, cols = {}, {}
    kern, dens, b0 = tile_call(
        pairs,
        ((0, 0),),
        rows,
        cols,
        part=0,
        moved=(base, up, down, over),
        swapped=(base_swapped, *cut(swapped)),
        fresh=(0,),
    )
    far_up, far_down, sides, dens = together(far_up, far_down, sides, dens)
    last_up = along(far_up[SUB : SUB + 128], 1)
    last_down = along(far_down[SUB : SUB + 128], -1)
    last = across(join(far_up[128:SUB], far_down[128:SUB]))
    swapped = swap(join(far_up, far_down, sides))
    more, dens, b1 = tile_call(
        pairs,
        ((0, 1),),
        rows,
        cols,
        old=dens,
        part=1,
        moved=(far_up, far_down, sides),
        swapped=cut(swapped),
        fresh=(1,),
    )
    kern.update(more)
    last_up, last_down, last, dens = together(last_up, last_down, last, dens)
    last_swapped = swap(join(last_up, last_down, last))
    more, dens = tile_call(pairs, ((1, 1), (1, 0)), rows, cols, old=dens)
    kern.update(more)
    last_swapped, dens = together(last_swapped, dens)
    more, dens, b2 = tile_call(
        pairs,
        ((0, 2), (1, 2), (2, 2), (2, 0), (2, 1)),
        rows,
        cols,
        old=dens,
        part=2,
        moved=(last_up, last_down, last),
        swapped=[last_swapped[k * 128 : (k + 1) * 128] for k in range(3)],
        fresh=(2,),
    )
    kern.update(more)

    t = dens + swap(dens)
    t = t + fetch(t, COL_PAIR)
    t = t + fetch(t, dict(z=lambda z: z ^ 1))
    keys = tuple(sorted(kern))
    blocks = [kern[k] for k in keys]
    there, density, *scaled = pl.pallas_call(
        functools.partial(scale_kernel, keys),
        in_specs=[VMEM] * 14,
        out_specs=[VMEM] * 5,
        out_shape=[f32(4, 24, SUB), f32(1, SUB)]
        + [jax.ShapeDtypeStruct((32, n), jnp.bfloat16) for n in N_COLS],
        scratch_shapes=[pltpu.VMEM((16, SUB), jnp.float32)],
        compiler_params=params(12),
        name="scale",
    )(t, fetch(t, dict(z=lambda z: 3 - z)), b0, b1, b2, *blocks)
    here = pl.pallas_call(
        functools.partial(here_kernel, keys),
        in_specs=[VMEM] * 12,
        out_specs=VMEM,
        out_shape=f32(4, 24, SUB),
        compiler_params=params(12),
        name="here",
    )(*scaled, *blocks)

    sums = here + fetch(there, ROW_PAIR)
    diffused = pl.pallas_call(
        finish,
        in_specs=[VMEM] * 4,
        out_specs=VMEM,
        out_shape=f32(16, SUB),
        compiler_params=params(8),
        name="finish",
    )(
        sums[0],
        fetch(sums[1], dict(x=-1)),
        fetch(sums[3], dict(x=1)),
        fetch(sums[2], dict(x=2)),
    )
    return diffused, density.reshape(SUB)


def solution(mesh):
    physical = Mesh(mesh.devices.reshape(SIZES), AXES)
    return jax.shard_map(
        body,
        mesh=physical,
        in_specs=(P(AXES, None), P(None, AXES), P()),
        out_specs=(P(None, AXES), P(AXES)),
        check_vma=False,
    )
```

```python
import functools
import math

import jax
import jax.numpy as jnp
from jax import lax
from jax.experimental import pallas as pl
from jax.experimental.pallas import tpu as pltpu
from jax.sharding import Mesh, PartitionSpec as P

D = 900
LANES = 1024
SUB = 192
CHUNK = 2 * SUB
WIDE = 256
AXES = ("ylo", "z", "core", "x", "yhi")
SIZES = (2, 4, 2, 4, 2)
SCALE = 2.0 * math.log2(math.e) / (0.25 * D)
NEG = -1e30
ROW_PAIR = dict(ylo=1)
COL_PAIR = dict(ylo=1, yhi=1)
CHIPS = ((0, 0), (1, 0), (3, 0), (0, 1), (2, 0), (1, 1), (3, 1), (2, 1))
ROWS = ((0, 1, 2, 3), (4, 5), (6, 7))
PARTS = tuple(tuple((chip, core) for chip in chips for core in (1, 0)) for chips in ROWS)
ROW_COPIES = (
    tuple(tuple((k, core * SUB, k * SUB, SUB) for k in range(4)) for core in (0, 1)),
    (
        ((0, 0, 0, 128), (1, 0, 128, 64), (0, 128, SUB, 128), (2, 0, SUB + 128, 64)),
        ((1, 64, 0, SUB), (2, 64, SUB, SUB)),
    ),
    (
        ((1, 0, 0, SUB), (0, 0, SUB, SUB)),
        ((1, SUB, 0, 64), (2, 0, 64, 128), (0, SUB, SUB, 64), (2, 128, SUB + 64, 128)),
    ),
)
COL_COPIES = (
    tuple((k, 0, k * CHUNK, CHUNK) for k in range(4)),
    ((0, 0, 0, 128), (1, 0, 128, 256), (0, 128, CHUNK, 128), (2, 0, CHUNK + 128, 256)),
    ((1, 0, 0, 256), (2, 0, 256, 128), (0, 0, CHUNK, 256), (2, 128, CHUNK + 256, 128)),
)
N_ROWS = tuple(len(r) * SUB for r in ROWS)
N_COLS = tuple(len(c) * SUB for c in PARTS)
VMEM = pl.BlockSpec(memory_space=pltpu.VMEM)
SMEM = pl.BlockSpec(memory_space=pltpu.SMEM)


def params(mib):
    return pltpu.CompilerParams(vmem_limit_bytes=mib * 2**20)


def fetch(array, first, second=None):
    pairs = []
    for dst in range(math.prod(SIZES)):
        rest, coords = dst, []
        for size in reversed(SIZES):
            coords.append(rest % size)
            rest //= size
        coords.reverse()
        delta = second if second is not None and coords[2] else first
        src = 0
        for axis, size, at in zip(AXES, SIZES, coords):
            by = delta.get(axis, 0)
            src = src * size + (by(at) if callable(by) else (at + by) % size)
        pairs.append((src, dst))
    return lax.ppermute(array, AXES, pairs)


def along(array, by):
    return fetch(array, dict(x=by), dict(z=by))


def across(array):
    return fetch(array, ROW_PAIR, COL_PAIR)


def swap(array):
    return fetch(array, dict(core=1))


def together(*arrays):
    return lax.optimization_barrier(arrays)


def forms(ref, basis_ref):
    lane = lax.broadcasted_iota(jnp.int32, (SUB, 128), 1)
    values = ref[...].astype(jnp.float32)
    sq = -0.5 * jnp.sum(values * values, axis=1, keepdims=True)
    high = sq.astype(jnp.bfloat16).astype(jnp.float32)
    mid = (sq - high).astype(jnp.bfloat16).astype(jnp.float32)
    low = (sq - high - mid).astype(jnp.bfloat16).astype(jnp.float32)
    tail = jnp.concatenate([values[:, 896:], jnp.zeros((SUB, 124), jnp.float32)], axis=1)
    basis = basis_ref[...].astype(jnp.float32)
    basis = jnp.concatenate([jnp.zeros((16, SUB)), basis, jnp.zeros((96, SUB))], axis=0).T

    def fill(first, ones_at, rest):
        out = jnp.where(lane == first, high, rest)
        out = jnp.where(lane == first + 1, mid, out)
        out = jnp.where(lane == first + 2, low, out)
        return jnp.where((lane >= ones_at) & (lane < ones_at + 3), 1.0, out)

    row_form, col_form = fill(4, 7, tail), fill(7, 4, tail + basis)
    is_first = lax.axis_index("core") == 0
    moved = jnp.where(is_first, row_form, col_form).astype(jnp.bfloat16)
    return moved, jnp.where(is_first, col_form, row_form).astype(jnp.bfloat16)


def prepare(coords_hbm, basis_hbm, out_ref, coords_ref, basis_ref, sems):
    copies = [
        pltpu.make_async_copy(coords_hbm, coords_ref, sems.at[0]),
        pltpu.make_async_copy(basis_hbm, basis_ref, sems.at[1]),
    ]
    for c in copies:
        c.start()
    for c in copies:
        c.wait()
    out_ref[:SUB, :896] = coords_ref[:, :896]
    out_ref[SUB:, :896] = coords_ref[:, :896]
    out_ref[:SUB, 896:], out_ref[SUB:, 896:] = forms(coords_ref, basis_ref)


def prepare_other(own_ref, coords_ref, basis_ref, base_ref, swapped_ref):
    base_ref[:SUB], swapped_ref[SUB:] = own_ref[:SUB], own_ref[SUB:]
    base_ref[SUB:, :896] = coords_ref[:, :896]
    swapped_ref[:SUB, :896] = coords_ref[:, :896]
    base_ref[SUB:, 896:], swapped_ref[:SUB, 896:] = forms(coords_ref, basis_ref)


def block_of(chip, core):
    dz, dyl = CHIPS[chip]
    ylo = lax.rem(lax.axis_index("ylo") + dyl, 2)
    return (ylo * 4 + lax.rem(lax.axis_index("z") + dz, 4)) * 2 + core


def start_all(plan, sems):
    copies = [
        pltpu.make_async_copy(src[k].at[pl.ds(at, n)], dst.at[pl.ds(to, n)], sems.at[sem])
        for sem, (src, dst, (k, at, to, n)) in enumerate(plan)
    ]
    for c in copies:
        c.start()
    for c in copies:
        c.wait()


def block_sums(r, rows, c, cols, out, pairs_ref, dens_ref, first=False):
    core = lax.axis_index("core")
    width = N_COLS[c]
    lane = lax.broadcasted_iota(jnp.int32, (1, width), 1)
    limits = {}
    for pair in sorted({CHIPS[k][1] for k in ROWS[r]}):
        limit = jnp.zeros((1, width), jnp.float32)
        for k, (chip, of) in enumerate(PARTS[c]):
            here = (lane >= k * SUB) & (lane < (k + 1) * SUB)
            live = pairs_ref[block_of(3 * pair, core), block_of(chip, of)] > 0
            limit = jnp.where(here, jnp.where(live, 0.0, NEG), limit)
        limits[pair] = limit
    totals = []
    for at in range(0, width, WIDE):
        ns = slice(at, at + WIDE)
        total = jnp.zeros((8, WIDE), jnp.float32)
        for m in range(0, N_ROWS[r], CHUNK):
            gram = lax.dot_general(
                rows[m : m + CHUNK, :],
                cols[ns, :],
                (((1,), (1,)), ((), ())),
                preferred_element_type=jnp.float32,
            )
            for k in range(CHUNK // SUB):
                limit = limits[CHIPS[ROWS[r][m // SUB + k]][1]][:, ns]
                kern = jnp.minimum(gram[k * SUB : (k + 1) * SUB] * SCALE, limit)
                kern = jnp.exp2(kern)
                out[m + k * SUB : m + (k + 1) * SUB, ns] = kern.astype(jnp.bfloat16)
                total += jnp.sum(kern.reshape(SUB // 8, 8, WIDE), axis=0)
        totals.append(jnp.sum(total, axis=0, keepdims=True))
    totals = jnp.concatenate(totals, axis=1)
    for k, (chip, of) in enumerate(PARTS[c]):
        row = pl.ds(block_of(chip, of), 1)
        total = totals[:, k * SUB : (k + 1) * SUB]
        dens_ref[row, :] = total if first else total + dens_ref[row, :]


def basis_of(cols):
    return cols[:, 896:].astype(jnp.float32).T[16:32].astype(jnp.bfloat16)


def pieces(ref, n):
    return [ref.at[pl.ds(k, n)] for k in range(0, ref.shape[0], n)]


def first_tile(pairs_ref, *refs):
    moved, (base_swapped, swapped, k00, dens, basis, rows, cols, sems) = refs[:4], refs[4:]
    swapped = [base_swapped] + pieces(swapped, CHUNK)
    for is_first in (True, False):

        @pl.when((lax.axis_index("core") == 0) == is_first)
        def _(is_first=is_first):
            row_from, col_from = (moved, swapped) if is_first else (swapped, moved)
            plan = [(row_from, rows, c) for c in ROW_COPIES[0][0 if is_first else 1]]
            start_all(plan + [(col_from, cols, c) for c in COL_COPIES[0]], sems)

    dens[...] = jnp.zeros_like(dens)
    block_sums(0, rows, 0, cols, k00, pairs_ref, dens, first=True)
    basis[...] = basis_of(cols)


def second_tile(pairs_ref, *refs):
    moved, swapped, refs = refs[:3], pieces(refs[3], 256), refs[4:]
    rows0, cols0, old, k01, k10, k11, dens, basis, rows, cols, sems = refs
    for is_first in (True, False):

        @pl.when((lax.axis_index("core") == 0) == is_first)
        def _(is_first=is_first):
            row_from, col_from = (moved, swapped) if is_first else (swapped, moved)
            plan = [(row_from, rows, c) for c in ROW_COPIES[1][0 if is_first else 1]]
            start_all(plan + [(col_from, cols, c) for c in COL_COPIES[1]], sems)

    dens[...] = old[...]
    block_sums(0, rows0, 1, cols, k01, pairs_ref, dens, first=True)
    block_sums(1, rows, 0, cols0, k10, pairs_ref, dens)
    block_sums(1, rows, 1, cols, k11, pairs_ref, dens)
    basis[...] = basis_of(cols)


def third_tile(pairs_ref, *refs):
    moved, refs = refs[:3], refs[3:]
    rows0, rows1, cols0, cols1, old, k20, k21, k02, k12, dens, held, sems = refs
    dens[...] = old[...]

    @pl.when(lax.axis_index("core") == 0)
    def _():
        start_all([(moved, held, c) for c in ROW_COPIES[2][0]], sems)
        rows = held.at[pl.ds(0, CHUNK)]
        block_sums(2, rows, 0, cols0, k20, pairs_ref, dens)
        block_sums(2, rows, 1, cols1, k21, pairs_ref, dens)

    @pl.when(lax.axis_index("core") == 1)
    def _():
        start_all([(moved, held, c) for c in COL_COPIES[2]], sems)
        block_sums(0, rows0, 2, held, k02, pairs_ref, dens)
        block_sums(1, rows1, 2, held, k12, pairs_ref, dens)


def fourth_tile(pairs_ref, *refs):
    swapped, refs = pieces(refs[0], 256), refs[1:]
    rows0, rows1, cols0, cols1, held, old, p20, p21, p02, p12 = refs[:10]
    k20, k21, k02, k12, k22, dens, basis, new, copy_sems, sems = refs[10:]
    dens[...] = old[...]

    def keep(*blocks):
        copies = [pltpu.make_async_copy(a, b, copy_sems.at[k]) for k, (a, b) in enumerate(blocks)]
        for c in copies:
            c.start()
        return copies

    @pl.when(lax.axis_index("core") == 0)
    def _():
        copies = keep((p20, k20), (p21, k21))
        start_all([(swapped, new, c) for c in COL_COPIES[2]], sems)
        block_sums(0, rows0, 2, new, k02, pairs_ref, dens)
        block_sums(1, rows1, 2, new, k12, pairs_ref, dens)
        block_sums(2, held.at[pl.ds(0, CHUNK)], 2, new, k22, pairs_ref, dens)
        basis[...] = basis_of(new)
        for c in copies:
            c.wait()

    @pl.when(lax.axis_index("core") == 1)
    def _():
        copies = keep((p02, k02), (p12, k12))
        start_all([(swapped, new, c) for c in ROW_COPIES[2][1]], sems)
        rows = new.at[pl.ds(0, CHUNK)]
        block_sums(2, rows, 0, cols0, k20, pairs_ref, dens)
        block_sums(2, rows, 1, cols1, k21, pairs_ref, dens)
        block_sums(2, rows, 2, held, k22, pairs_ref, dens)
        basis[...] = basis_of(held)
        for c in copies:
            c.wait()


def tile_call(kernel, pairs, operands, blocks, others, scratch=()):
    units = sum(N_ROWS[r] * N_COLS[c] for r, c in blocks)
    result = pl.pallas_call(
        kernel,
        in_specs=[SMEM] + [VMEM] * len(operands),
        out_specs=[VMEM] * (len(blocks) + len(others)),
        out_shape=[jax.ShapeDtypeStruct((N_ROWS[r], N_COLS[c]), jnp.bfloat16) for r, c in blocks]
        + [jax.ShapeDtypeStruct(*o) for o in others],
        scratch_shapes=[*scratch, pltpu.SemaphoreType.DMA((8,))],
        compiler_params=params(12),
        cost_estimate=pl.CostEstimate(flops=units, bytes_accessed=units, transcendentals=0),
        name=kernel.__name__,
    )(pairs, *operands)
    return dict(zip(blocks, result)), *result[len(blocks) :]


def scale_kernel(keys, t0, t1, b0, b1, b2, *refs):
    kern, refs = dict(zip(keys, refs)), refs[len(keys) :]
    there_ref, here_ref, density_ref, inv, s0, s1, s2 = refs
    total = t0[...] + t1[...]
    inv[...] = total
    density_ref[...] = inv[pl.ds(block_of(0, lax.axis_index("core")), 1), :]
    inv[...] = 1.0 / total
    for part, basis, scaled in zip(PARTS, (b0, b1, b2), (s0, s1, s2)):
        inverse = jnp.concatenate([inv[pl.ds(block_of(*s), 1), :] for s in part], axis=1)
        first = lax.broadcasted_iota(jnp.int32, (16, inverse.shape[1]), 0) == 0
        scaled[:16, :] = (basis[...].astype(jnp.float32) * inverse).astype(jnp.bfloat16)
        scaled[16:, :] = jnp.where(first, inverse, 0.0).astype(jnp.bfloat16)
    row_sums(1, (s0, s1, s2), kern, there_ref)
    row_sums(0, (s0, s1, s2), kern, here_ref)


def row_sums(pair, scaled, kern, out_ref):
    for r in range(3):
        at = [k for k, chip in enumerate(ROWS[r]) if CHIPS[chip][1] == pair]
        if not at:
            continue
        ms = slice(at[0] * SUB, (at[-1] + 1) * SUB)
        both = sum(
            lax.dot_general(
                s[...],
                kern[r, c][ms, :],
                (((1,), (1,)), ((), ())),
                preferred_element_type=jnp.float32,
            )
            for c, s in enumerate(scaled)
        )
        for k in at:
            part = both[:24, (k - at[0]) * SUB : (k - at[0] + 1) * SUB]
            out_ref[CHIPS[ROWS[r][k]][0]] = part


def finish(a_ref, b_ref, c_ref, d_ref, out_ref):
    total = a_ref[...] + b_ref[...] + c_ref[...] + d_ref[...]
    out_ref[...] = total[:16] / total[16:17]


def body(coords, basis, pairs):
    f32 = lambda *s: jax.ShapeDtypeStruct(s, jnp.float32)
    form = lambda *s: jax.ShapeDtypeStruct((CHUNK, LANES), jnp.bfloat16)
    own = pl.pallas_call(
        prepare,
        in_specs=[pl.BlockSpec(memory_space=pltpu.HBM)] * 2,
        out_specs=VMEM,
        out_shape=form(),
        scratch_shapes=[
            pltpu.VMEM((SUB, D), jnp.bfloat16),
            pltpu.VMEM((16, SUB), jnp.bfloat16),
            pltpu.SemaphoreType.DMA((2,)),
        ],
        compiler_params=params(8),
        name="prepare",
    )(coords, basis)
    base, base_swapped = pl.pallas_call(
        prepare_other,
        in_specs=[VMEM] * 3,
        out_specs=[VMEM] * 2,
        out_shape=[form(), form()],
        compiler_params=params(8),
        name="prepare_other",
    )(own, swap(coords), swap(basis))
    join = lambda *arrays: jnp.concatenate(arrays)
    sums = ((16, SUB), jnp.float32)
    basis_cols = [((16, n), jnp.bfloat16) for n in N_COLS]
    frames = lambda n: ((n, LANES), jnp.bfloat16)

    up, down, over = together(along(base, 1), along(base, -1), across(base))
    a1 = along(join(up[:128], over[:128]), 1)
    a2 = along(down[128:], -1)
    a3 = across(up[128:])
    swapped = swap(join(up, down, over))
    kern, dens, b0, rows0, cols0 = tile_call(
        first_tile,
        pairs,
        (base, up, down, over, base_swapped, swapped),
        ((0, 0),),
        (sums, basis_cols[0], frames(N_ROWS[0]), frames(N_COLS[0])),
    )
    a1, a2, a3, dens, over, down = together(a1, a2, a3, dens, over, down)
    z1 = along(join(a1[128:], a3[:128]), 1)
    z2 = along(over[:256], -1)
    z3 = across(join(down[256:], a2[128:]))
    swapped = swap(join(a1, a2, a3))
    more, dens, b1, rows1, cols1 = tile_call(
        second_tile,
        pairs,
        (a1, a2, a3, swapped, rows0, cols0, dens),
        ((0, 1), (1, 0), (1, 1)),
        (sums, basis_cols[1], frames(N_ROWS[1]), frames(N_COLS[1])),
    )
    kern.update(more)
    z1, z2, z3, dens = together(z1, z2, z3, dens)
    swapped = swap(join(z1, z2, z3))
    blocks = ((2, 0), (2, 1), (0, 2), (1, 2))
    more, dens, held = tile_call(
        third_tile,
        pairs,
        (z1, z2, z3, rows0, rows1, cols0, cols1, dens),
        blocks,
        (sums, frames(N_COLS[2])),
    )
    more, dens, b2 = tile_call(
        fourth_tile,
        pairs,
        (swapped, rows0, rows1, cols0, cols1, held, dens, *[more[k] for k in blocks]),
        blocks + ((2, 2),),
        (sums, basis_cols[2]),
        [pltpu.VMEM((N_COLS[2], LANES), jnp.bfloat16), pltpu.SemaphoreType.DMA((2,))],
    )
    kern.update(more)

    t = dens + swap(dens)
    t = t + fetch(t, dict(COL_PAIR, core=1))
    t = t + fetch(t, dict(z=lambda z: z ^ 1, core=1))
    keys = tuple(sorted(kern))
    blocks = [kern[k] for k in keys]
    there, here, density = pl.pallas_call(
        functools.partial(scale_kernel, keys),
        in_specs=[VMEM] * 14,
        out_specs=[VMEM] * 3,
        out_shape=[f32(4, 24, SUB), f32(4, 24, SUB), f32(1, SUB)],
        scratch_shapes=[pltpu.VMEM((16, SUB), jnp.float32)]
        + [pltpu.VMEM((32, n), jnp.bfloat16) for n in N_COLS],
        compiler_params=params(12),
        name="scale",
    )(t, fetch(t, dict(z=lambda z: 3 - z, core=1)), b0, b1, b2, *blocks)

    total = swap(here) + fetch(there, dict(ROW_PAIR, core=1))
    diffused = pl.pallas_call(
        finish,
        in_specs=[VMEM] * 4,
        out_specs=VMEM,
        out_shape=f32(16, SUB),
        compiler_params=params(8),
        name="finish",
    )(
        swap(total[0]),
        fetch(total[1], dict(x=-1, core=1)),
        fetch(total[3], dict(x=1, core=1)),
        fetch(total[2], dict(x=2, core=1)),
    )
    return diffused, density.reshape(SUB)


def solution(mesh):
    physical = Mesh(mesh.devices.reshape(SIZES), AXES)
    return jax.shard_map(
        body,
        mesh=physical,
        in_specs=(P(AXES, None), P(None, AXES), P()),
        out_specs=(P(None, AXES), P(AXES)),
        check_vma=False,
    )
```

```python
import functools
import math

import jax
import jax.numpy as jnp
from jax import lax
from jax.experimental import pallas as pl
from jax.experimental.pallas import tpu as pltpu
from jax.sharding import Mesh, PartitionSpec as P

D = 900
LANES = 1024
SUB = 192
CHUNK = 2 * SUB
WIDE = 256
AXES = ("ylo", "z", "core", "x", "yhi")
SIZES = (2, 4, 2, 4, 2)
SCALE = 2.0 * math.log2(math.e) / (0.25 * D)
NEG = -1e30
ROW_PAIR = dict(ylo=1)
COL_PAIR = dict(ylo=1, yhi=1)
CHIPS = ((0, 0), (1, 0), (3, 0), (0, 1), (2, 0), (1, 1), (3, 1), (2, 1))
ROWS = ((0, 1, 2, 3), (4, 5), (6, 7))
PARTS = tuple(tuple((chip, core) for chip in chips for core in (1, 0)) for chips in ROWS)
ROW_COPIES = (
    tuple(tuple((k, core * SUB, k * SUB, SUB) for k in range(4)) for core in (0, 1)),
    (
        ((0, 0, 0, 128), (1, 0, 128, 64), (0, 128, SUB, 128), (2, 0, SUB + 128, 64)),
        ((1, 64, 0, SUB), (2, 64, SUB, SUB)),
    ),
    (
        ((1, 0, 0, SUB), (0, 0, SUB, SUB)),
        ((1, SUB, 0, 64), (2, 0, 64, 128), (0, SUB, SUB, 64), (2, 128, SUB + 64, 128)),
    ),
)
COL_COPIES = (
    tuple((k, 0, k * CHUNK, CHUNK) for k in range(4)),
    ((0, 0, 0, 128), (1, 0, 128, 256), (0, 128, CHUNK, 128), (2, 0, CHUNK + 128, 256)),
    ((1, 0, 0, 256), (2, 0, 256, 128), (0, 0, CHUNK, 256), (2, 128, CHUNK + 256, 128)),
)
N_ROWS = tuple(len(r) * SUB for r in ROWS)
N_COLS = tuple(len(c) * SUB for c in PARTS)
VMEM = pl.BlockSpec(memory_space=pltpu.VMEM)
SMEM = pl.BlockSpec(memory_space=pltpu.SMEM)


def params(mib):
    return pltpu.CompilerParams(vmem_limit_bytes=mib * 2**20)


def fetch(array, first, second=None):
    pairs = []
    for dst in range(math.prod(SIZES)):
        rest, coords = dst, []
        for size in reversed(SIZES):
            coords.append(rest % size)
            rest //= size
        coords.reverse()
        delta = second if second is not None and coords[2] else first
        src = 0
        for axis, size, at in zip(AXES, SIZES, coords):
            by = delta.get(axis, 0)
            src = src * size + (by(at) if callable(by) else (at + by) % size)
        pairs.append((src, dst))
    return lax.ppermute(array, AXES, pairs)


def along(array, by):
    return fetch(array, dict(x=by), dict(z=by))


def across(array):
    return fetch(array, ROW_PAIR, COL_PAIR)


def swap(array):
    return fetch(array, dict(core=1))


def together(*arrays):
    return lax.optimization_barrier(arrays)


def forms(ref, basis_ref):
    lane = lax.broadcasted_iota(jnp.int32, (SUB, 128), 1)
    values = ref[...].astype(jnp.float32)
    sq = -0.5 * jnp.sum(values * values, axis=1, keepdims=True)
    high = sq.astype(jnp.bfloat16).astype(jnp.float32)
    mid = (sq - high).astype(jnp.bfloat16).astype(jnp.float32)
    low = (sq - high - mid).astype(jnp.bfloat16).astype(jnp.float32)
    tail = jnp.concatenate([values[:, 896:], jnp.zeros((SUB, 124), jnp.float32)], axis=1)
    basis = basis_ref[...].astype(jnp.float32)
    basis = jnp.concatenate([jnp.zeros((16, SUB)), basis, jnp.zeros((96, SUB))], axis=0).T

    def fill(first, ones_at, rest):
        out = jnp.where(lane == first, high, rest)
        out = jnp.where(lane == first + 1, mid, out)
        out = jnp.where(lane == first + 2, low, out)
        return jnp.where((lane >= ones_at) & (lane < ones_at + 3), 1.0, out)

    row_form, col_form = fill(4, 7, tail), fill(7, 4, tail + basis)
    is_first = lax.axis_index("core") == 0
    moved = jnp.where(is_first, row_form, col_form).astype(jnp.bfloat16)
    return moved, jnp.where(is_first, col_form, row_form).astype(jnp.bfloat16)


def prepare(coords_hbm, basis_hbm, out_ref, coords_ref, basis_ref, sems):
    copies = [
        pltpu.make_async_copy(coords_hbm, coords_ref, sems.at[0]),
        pltpu.make_async_copy(basis_hbm, basis_ref, sems.at[1]),
    ]
    for c in copies:
        c.start()
    for c in copies:
        c.wait()
    out_ref[:SUB, :896] = coords_ref[:, :896]
    out_ref[SUB:, :896] = coords_ref[:, :896]
    out_ref[:SUB, 896:], out_ref[SUB:, 896:] = forms(coords_ref, basis_ref)


def prepare_other(own_ref, coords_ref, basis_ref, base_ref, swapped_ref):
    base_ref[:SUB], swapped_ref[SUB:] = own_ref[:SUB], own_ref[SUB:]
    base_ref[SUB:, :896] = coords_ref[:, :896]
    swapped_ref[:SUB, :896] = coords_ref[:, :896]
    base_ref[SUB:, 896:], swapped_ref[:SUB, 896:] = forms(coords_ref, basis_ref)


def block_of(chip, core):
    dz, dyl = CHIPS[chip]
    ylo = lax.rem(lax.axis_index("ylo") + dyl, 2)
    return (ylo * 4 + lax.rem(lax.axis_index("z") + dz, 4)) * 2 + core


def start_all(plan, sems):
    copies = [
        pltpu.make_async_copy(src[k].at[pl.ds(at, n)], dst.at[pl.ds(to, n)], sems.at[sem])
        for sem, (src, dst, (k, at, to, n)) in enumerate(plan)
    ]
    for c in copies:
        c.start()
    for c in copies:
        c.wait()


def block_sums(r, rows, c, cols, out, pairs_ref, dens_ref, first=False):
    core = lax.axis_index("core")
    width = N_COLS[c]
    lane = lax.broadcasted_iota(jnp.int32, (1, width), 1)
    limits = {}
    for pair in sorted({CHIPS[k][1] for k in ROWS[r]}):
        limit = jnp.zeros((1, width), jnp.float32)
        for k, (chip, of) in enumerate(PARTS[c]):
            here = (lane >= k * SUB) & (lane < (k + 1) * SUB)
            live = pairs_ref[block_of(3 * pair, core), block_of(chip, of)] > 0
            limit = jnp.where(here, jnp.where(live, 0.0, NEG), limit)
        limits[pair] = limit
    totals = []
    for at in range(0, width, WIDE):
        ns = slice(at, at + WIDE)
        total = jnp.zeros((8, WIDE), jnp.float32)
        for m in range(0, N_ROWS[r], CHUNK):
            gram = lax.dot_general(
                rows[m : m + CHUNK, :],
                cols[ns, :],
                (((1,), (1,)), ((), ())),
                preferred_element_type=jnp.float32,
            )
            for k in range(CHUNK // SUB):
                limit = limits[CHIPS[ROWS[r][m // SUB + k]][1]][:, ns]
                kern = jnp.minimum(gram[k * SUB : (k + 1) * SUB] * SCALE, limit)
                kern = jnp.exp2(kern)
                out[m + k * SUB : m + (k + 1) * SUB, ns] = kern.astype(jnp.bfloat16)
                total += jnp.sum(kern.reshape(SUB // 8, 8, WIDE), axis=0)
        totals.append(jnp.sum(total, axis=0, keepdims=True))
    totals = jnp.concatenate(totals, axis=1)
    for k, (chip, of) in enumerate(PARTS[c]):
        row = pl.ds(block_of(chip, of), 1)
        total = totals[:, k * SUB : (k + 1) * SUB]
        dens_ref[row, :] = total if first else total + dens_ref[row, :]


def basis_of(cols):
    return cols[:, 896:].astype(jnp.float32).T[16:32].astype(jnp.bfloat16)


def pieces(ref, n):
    return [ref.at[pl.ds(k, n)] for k in range(0, ref.shape[0], n)]


def first_tile(pairs_ref, *refs):
    moved, (base_swapped, swapped, k00, dens, basis, rows, cols, sems) = refs[:4], refs[4:]
    swapped = [base_swapped] + pieces(swapped, CHUNK)
    for is_first in (True, False):

        @pl.when((lax.axis_index("core") == 0) == is_first)
        def _(is_first=is_first):
            row_from, col_from = (moved, swapped) if is_first else (swapped, moved)
            plan = [(row_from, rows, c) for c in ROW_COPIES[0][0 if is_first else 1]]
            start_all(plan + [(col_from, cols, c) for c in COL_COPIES[0]], sems)

    dens[...] = jnp.zeros_like(dens)
    block_sums(0, rows, 0, cols, k00, pairs_ref, dens, first=True)
    basis[...] = basis_of(cols)


def second_tile(pairs_ref, *refs):
    moved, swapped, refs = refs[:3], pieces(refs[3], 256), refs[4:]
    rows0, cols0, old, k01, k10, k11, dens, basis, rows, cols, sems = refs
    for is_first in (True, False):

        @pl.when((lax.axis_index("core") == 0) == is_first)
        def _(is_first=is_first):
            row_from, col_from = (moved, swapped) if is_first else (swapped, moved)
            plan = [(row_from, rows, c) for c in ROW_COPIES[1][0 if is_first else 1]]
            start_all(plan + [(col_from, cols, c) for c in COL_COPIES[1]], sems)

    dens[...] = old[...]
    block_sums(0, rows0, 1, cols, k01, pairs_ref, dens, first=True)
    block_sums(1, rows, 0, cols0, k10, pairs_ref, dens)
    block_sums(1, rows, 1, cols, k11, pairs_ref, dens)
    basis[...] = basis_of(cols)


def third_tile(pairs_ref, *refs):
    moved, refs = refs[:3], refs[3:]
    rows0, rows1, cols0, cols1, old, k20, k21, k02, k12, dens, held, sems = refs
    dens[...] = old[...]

    @pl.when(lax.axis_index("core") == 0)
    def _():
        start_all([(moved, held, c) for c in ROW_COPIES[2][0]], sems)
        rows = held.at[pl.ds(0, CHUNK)]
        block_sums(2, rows, 0, cols0, k20, pairs_ref, dens)
        block_sums(2, rows, 1, cols1, k21, pairs_ref, dens)

    @pl.when(lax.axis_index("core") == 1)
    def _():
        start_all([(moved, held, c) for c in COL_COPIES[2]], sems)
        block_sums(0, rows0, 2, held, k02, pairs_ref, dens)
        block_sums(1, rows1, 2, held, k12, pairs_ref, dens)


def fourth_tile(pairs_ref, *refs):
    swapped, refs = pieces(refs[0], 256), refs[1:]
    rows0, rows1, cols0, cols1, held, old, p20, p21, p02, p12 = refs[:10]
    k20, k21, k02, k12, k22, dens, basis, new, copy_sems, sems = refs[10:]
    dens[...] = old[...]

    def keep(*blocks):
        copies = [pltpu.make_async_copy(a, b, copy_sems.at[k]) for k, (a, b) in enumerate(blocks)]
        for c in copies:
            c.start()
        return copies

    @pl.when(lax.axis_index("core") == 0)
    def _():
        copies = keep((p20, k20), (p21, k21))
        start_all([(swapped, new, c) for c in COL_COPIES[2]], sems)
        block_sums(0, rows0, 2, new, k02, pairs_ref, dens)
        block_sums(1, rows1, 2, new, k12, pairs_ref, dens)
        block_sums(2, held.at[pl.ds(0, CHUNK)], 2, new, k22, pairs_ref, dens)
        basis[...] = basis_of(new)
        for c in copies:
            c.wait()

    @pl.when(lax.axis_index("core") == 1)
    def _():
        copies = keep((p02, k02), (p12, k12))
        start_all([(swapped, new, c) for c in ROW_COPIES[2][1]], sems)
        rows = new.at[pl.ds(0, CHUNK)]
        block_sums(2, rows, 0, cols0, k20, pairs_ref, dens)
        block_sums(2, rows, 1, cols1, k21, pairs_ref, dens)
        block_sums(2, rows, 2, held, k22, pairs_ref, dens)
        basis[...] = basis_of(held)
        for c in copies:
            c.wait()


def tile_call(kernel, pairs, operands, blocks, others, scratch=()):
    units = sum(N_ROWS[r] * N_COLS[c] for r, c in blocks)
    result = pl.pallas_call(
        kernel,
        in_specs=[SMEM] + [VMEM] * len(operands),
        out_specs=[VMEM] * (len(blocks) + len(others)),
        out_shape=[jax.ShapeDtypeStruct((N_ROWS[r], N_COLS[c]), jnp.bfloat16) for r, c in blocks]
        + [jax.ShapeDtypeStruct(*o) for o in others],
        scratch_shapes=[*scratch, pltpu.SemaphoreType.DMA((8,))],
        compiler_params=params(12),
        cost_estimate=pl.CostEstimate(flops=units, bytes_accessed=units, transcendentals=0),
        name=kernel.__name__,
    )(pairs, *operands)
    return dict(zip(blocks, result)), *result[len(blocks) :]


def scale_kernel(keys, t0, t1, b0, b1, b2, *refs):
    kern, refs = dict(zip(keys, refs)), refs[len(keys) :]
    there_ref, here_ref, density_ref, inv, s0, s1, s2 = refs
    total = t0[...] + t1[...]
    inv[...] = total
    density_ref[...] = inv[pl.ds(block_of(0, lax.axis_index("core")), 1), :]
    inv[...] = 1.0 / total
    for part, basis, scaled in zip(PARTS, (b0, b1, b2), (s0, s1, s2)):
        inverse = jnp.concatenate([inv[pl.ds(block_of(*s), 1), :] for s in part], axis=1)
        first = lax.broadcasted_iota(jnp.int32, (16, inverse.shape[1]), 0) == 0
        scaled[:16, :] = (basis[...].astype(jnp.float32) * inverse).astype(jnp.bfloat16)
        scaled[16:, :] = jnp.where(first, inverse, 0.0).astype(jnp.bfloat16)
    row_sums(1, (s0, s1, s2), kern, there_ref)
    row_sums(0, (s0, s1, s2), kern, here_ref)


def row_sums(pair, scaled, kern, out_ref):
    for r in range(3):
        at = [k for k, chip in enumerate(ROWS[r]) if CHIPS[chip][1] == pair]
        if not at:
            continue
        ms = slice(at[0] * SUB, (at[-1] + 1) * SUB)
        both = sum(
            lax.dot_general(
                s[...],
                kern[r, c][ms, :],
                (((1,), (1,)), ((), ())),
                preferred_element_type=jnp.float32,
            )
            for c, s in enumerate(scaled)
        )
        for k in at:
            part = both[:24, (k - at[0]) * SUB : (k - at[0] + 1) * SUB]
            out_ref[CHIPS[ROWS[r][k]][0]] = part


def finish(a_ref, b_ref, c_ref, d_ref, out_ref):
    total = a_ref[...] + b_ref[...] + c_ref[...] + d_ref[...]
    out_ref[...] = total[:16] / total[16:17]


def body(coords, basis, pairs):
    f32 = lambda *s: jax.ShapeDtypeStruct(s, jnp.float32)
    form = lambda *s: jax.ShapeDtypeStruct((CHUNK, LANES), jnp.bfloat16)
    own = pl.pallas_call(
        prepare,
        in_specs=[pl.BlockSpec(memory_space=pltpu.HBM)] * 2,
        out_specs=VMEM,
        out_shape=form(),
        scratch_shapes=[
            pltpu.VMEM((SUB, D), jnp.bfloat16),
            pltpu.VMEM((16, SUB), jnp.bfloat16),
            pltpu.SemaphoreType.DMA((2,)),
        ],
        compiler_params=params(8),
        name="prepare",
    )(coords, basis)
    base, base_swapped = pl.pallas_call(
        prepare_other,
        in_specs=[VMEM] * 3,
        out_specs=[VMEM] * 2,
        out_shape=[form(), form()],
        compiler_params=params(8),
        name="prepare_other",
    )(own, swap(coords), swap(basis))
    join = lambda *arrays: jnp.concatenate(arrays)
    sums = ((16, SUB), jnp.float32)
    basis_cols = [((16, n), jnp.bfloat16) for n in N_COLS]
    frames = lambda n: ((n, LANES), jnp.bfloat16)

    over = across(base)
    down = along(base, -1)
    up = along(base, 1)
    over, down, up = together(over, down, up)
    swapped = swap(join(up, down, over))
    a3 = across(up[128:])
    a2 = along(down[128:], -1)
    a1 = along(join(up[:128], over[:128]), 1)
    kern, dens, b0, rows0, cols0 = tile_call(
        first_tile,
        pairs,
        (base, up, down, over, base_swapped, swapped),
        ((0, 0),),
        (sums, basis_cols[0], frames(N_ROWS[0]), frames(N_COLS[0])),
    )
    dens, a3, a2, a1, over, down = together(dens, a3, a2, a1, over, down)
    swapped = swap(join(a1, a2, a3))
    z3 = across(join(down[256:], a2[128:]))
    z2 = along(over[:256], -1)
    z1 = along(join(a1[128:], a3[:128]), 1)
    more, dens, b1, rows1, cols1 = tile_call(
        second_tile,
        pairs,
        (a1, a2, a3, swapped, rows0, cols0, dens),
        ((0, 1), (1, 0), (1, 1)),
        (sums, basis_cols[1], frames(N_ROWS[1]), frames(N_COLS[1])),
    )
    kern.update(more)
    dens, z3, z2, z1 = together(dens, z3, z2, z1)
    swapped = swap(join(z1, z2, z3))
    blocks = ((2, 0), (2, 1), (0, 2), (1, 2))
    more, dens, held = tile_call(
        third_tile,
        pairs,
        (z1, z2, z3, rows0, rows1, cols0, cols1, dens),
        blocks,
        (sums, frames(N_COLS[2])),
    )
    more, dens, b2 = tile_call(
        fourth_tile,
        pairs,
        (swapped, rows0, rows1, cols0, cols1, held, dens, *[more[k] for k in blocks]),
        blocks + ((2, 2),),
        (sums, basis_cols[2]),
        [pltpu.VMEM((N_COLS[2], LANES), jnp.bfloat16), pltpu.SemaphoreType.DMA((2,))],
    )
    kern.update(more)

    t = dens + swap(dens)
    t = t + fetch(t, dict(COL_PAIR, core=1))
    t = t + fetch(t, dict(z=lambda z: z ^ 1, core=1))
    keys = tuple(sorted(kern))
    blocks = [kern[k] for k in keys]
    there, here, density = pl.pallas_call(
        functools.partial(scale_kernel, keys),
        in_specs=[VMEM] * 14,
        out_specs=[VMEM] * 3,
        out_shape=[f32(4, 24, SUB), f32(4, 24, SUB), f32(1, SUB)],
        scratch_shapes=[pltpu.VMEM((16, SUB), jnp.float32)]
        + [pltpu.VMEM((32, n), jnp.bfloat16) for n in N_COLS],
        compiler_params=params(12),
        name="scale",
    )(t, fetch(t, dict(z=lambda z: 3 - z, core=1)), b0, b1, b2, *blocks)

    total = swap(here) + fetch(there, dict(ROW_PAIR, core=1))
    diffused = pl.pallas_call(
        finish,
        in_specs=[VMEM] * 4,
        out_specs=VMEM,
        out_shape=f32(16, SUB),
        compiler_params=params(8),
        name="finish",
    )(
        swap(total[0]),
        fetch(total[1], dict(x=-1, core=1)),
        fetch(total[3], dict(x=1, core=1)),
        fetch(total[2], dict(x=2, core=1)),
    )
    return diffused, density.reshape(SUB)


def solution(mesh):
    physical = Mesh(mesh.devices.reshape(SIZES), AXES)
    return jax.shard_map(
        body,
        mesh=physical,
        in_specs=(P(AXES, None), P(None, AXES), P()),
        out_specs=(P(None, AXES), P(AXES)),
        check_vma=False,
    )
```

```python
import functools
import math

import jax
import jax.numpy as jnp
from jax import lax
from jax.experimental import pallas as pl
from jax.experimental.pallas import tpu as pltpu
from jax.sharding import Mesh, PartitionSpec as P

D = 900
LANES = 1024
SUB = 192
CHUNK = 2 * SUB
WIDE = 256
AXES = ("ylo", "z", "core", "x", "yhi")
SIZES = (2, 4, 2, 4, 2)
SCALE = 2.0 * math.log2(math.e) / (0.25 * D)
NEG = -1e30
ROW_PAIR = dict(ylo=1)
COL_PAIR = dict(ylo=1, yhi=1)
CHIPS = ((0, 0), (1, 0), (3, 0), (0, 1), (2, 0), (1, 1), (3, 1), (2, 1))
ROWS = ((0, 1, 2, 3), (4, 5), (6, 7))
PARTS = tuple(tuple((chip, core) for chip in chips for core in (1, 0)) for chips in ROWS)
ROW_COPIES = (
    tuple(tuple((k, core * SUB, k * SUB, SUB) for k in range(4)) for core in (0, 1)),
    (
        ((0, 0, 0, 128), (1, 0, 128, 64), (0, 128, SUB, 128), (2, 0, SUB + 128, 64)),
        ((1, 64, 0, SUB), (2, 64, SUB, SUB)),
    ),
    (
        ((1, 0, 0, SUB), (0, 0, SUB, SUB)),
        ((1, SUB, 0, 64), (2, 0, 64, 128), (0, SUB, SUB, 64), (2, 128, SUB + 64, 128)),
    ),
)
COL_COPIES = (
    tuple((k, 0, k * CHUNK, CHUNK) for k in range(4)),
    ((0, 0, 0, 128), (1, 0, 128, 256), (0, 128, CHUNK, 128), (2, 0, CHUNK + 128, 256)),
    ((1, 0, 0, 256), (2, 0, 256, 128), (0, 0, CHUNK, 256), (2, 128, CHUNK + 256, 128)),
)
N_ROWS = tuple(len(r) * SUB for r in ROWS)
N_COLS = tuple(len(c) * SUB for c in PARTS)
VMEM = pl.BlockSpec(memory_space=pltpu.VMEM)
SMEM = pl.BlockSpec(memory_space=pltpu.SMEM)


def params(mib):
    return pltpu.CompilerParams(vmem_limit_bytes=mib * 2**20)


def fetch(array, first, second=None):
    pairs = []
    for dst in range(math.prod(SIZES)):
        rest, coords = dst, []
        for size in reversed(SIZES):
            coords.append(rest % size)
            rest //= size
        coords.reverse()
        delta = second if second is not None and coords[2] else first
        src = 0
        for axis, size, at in zip(AXES, SIZES, coords):
            by = delta.get(axis, 0)
            src = src * size + (by(at) if callable(by) else (at + by) % size)
        pairs.append((src, dst))
    return lax.ppermute(array, AXES, pairs)


def along(array, by):
    return fetch(array, dict(x=by), dict(z=by))


def across(array):
    return fetch(array, ROW_PAIR, COL_PAIR)


def swap(array):
    return fetch(array, dict(core=1))


def together(*arrays):
    return lax.optimization_barrier(arrays)


def forms(ref, basis_ref):
    lane = lax.broadcasted_iota(jnp.int32, (SUB, 128), 1)
    values = ref[...].astype(jnp.float32)
    sq = -0.5 * jnp.sum(values * values, axis=1, keepdims=True)
    high = sq.astype(jnp.bfloat16).astype(jnp.float32)
    mid = (sq - high).astype(jnp.bfloat16).astype(jnp.float32)
    low = (sq - high - mid).astype(jnp.bfloat16).astype(jnp.float32)
    tail = jnp.concatenate([values[:, 896:], jnp.zeros((SUB, 124), jnp.float32)], axis=1)
    basis = basis_ref[...].astype(jnp.float32)
    basis = jnp.concatenate([jnp.zeros((16, SUB)), basis, jnp.zeros((96, SUB))], axis=0).T

    def fill(first, ones_at, rest):
        out = jnp.where(lane == first, high, rest)
        out = jnp.where(lane == first + 1, mid, out)
        out = jnp.where(lane == first + 2, low, out)
        return jnp.where((lane >= ones_at) & (lane < ones_at + 3), 1.0, out)

    row_form, col_form = fill(4, 7, tail), fill(7, 4, tail + basis)
    is_first = lax.axis_index("core") == 0
    moved = jnp.where(is_first, row_form, col_form).astype(jnp.bfloat16)
    return moved, jnp.where(is_first, col_form, row_form).astype(jnp.bfloat16)


def prepare(coords_hbm, basis_hbm, out_ref, coords_ref, basis_ref, sems):
    copies = [
        pltpu.make_async_copy(coords_hbm, coords_ref, sems.at[0]),
        pltpu.make_async_copy(basis_hbm, basis_ref, sems.at[1]),
    ]
    for c in copies:
        c.start()
    for c in copies:
        c.wait()
    out_ref[:SUB, :896] = coords_ref[:, :896]
    out_ref[SUB:, :896] = coords_ref[:, :896]
    out_ref[:SUB, 896:], out_ref[SUB:, 896:] = forms(coords_ref, basis_ref)


def prepare_other(own_ref, coords_ref, basis_ref, base_ref, swapped_ref):
    base_ref[:SUB], swapped_ref[SUB:] = own_ref[:SUB], own_ref[SUB:]
    base_ref[SUB:, :896] = coords_ref[:, :896]
    swapped_ref[:SUB, :896] = coords_ref[:, :896]
    base_ref[SUB:, 896:], swapped_ref[:SUB, 896:] = forms(coords_ref, basis_ref)


def block_of(chip, core):
    dz, dyl = CHIPS[chip]
    ylo = lax.rem(lax.axis_index("ylo") + dyl, 2)
    return (ylo * 4 + lax.rem(lax.axis_index("z") + dz, 4)) * 2 + core


def start_all(plan, sems):
    copies = [
        pltpu.make_async_copy(src[k].at[pl.ds(at, n)], dst.at[pl.ds(to, n)], sems.at[sem])
        for sem, (src, dst, (k, at, to, n)) in enumerate(plan)
    ]
    for c in copies:
        c.start()
    for c in copies:
        c.wait()


def block_sums(r, rows, c, cols, out, pairs_ref, dens_ref, first=False):
    core = lax.axis_index("core")
    width = N_COLS[c]
    lane = lax.broadcasted_iota(jnp.int32, (1, width), 1)
    limits = {}
    for pair in sorted({CHIPS[k][1] for k in ROWS[r]}):
        limit = jnp.zeros((1, width), jnp.float32)
        for k, (chip, of) in enumerate(PARTS[c]):
            here = (lane >= k * SUB) & (lane < (k + 1) * SUB)
            live = pairs_ref[block_of(3 * pair, core), block_of(chip, of)] > 0
            limit = jnp.where(here, jnp.where(live, 0.0, NEG), limit)
        limits[pair] = limit
    totals = []
    for at in range(0, width, WIDE):
        ns = slice(at, at + WIDE)
        total = jnp.zeros((8, WIDE), jnp.float32)
        for m in range(0, N_ROWS[r], CHUNK):
            gram = lax.dot_general(
                rows[m : m + CHUNK, :],
                cols[ns, :],
                (((1,), (1,)), ((), ())),
                preferred_element_type=jnp.float32,
            )
            for k in range(CHUNK // SUB):
                limit = limits[CHIPS[ROWS[r][m // SUB + k]][1]][:, ns]
                kern = jnp.minimum(gram[k * SUB : (k + 1) * SUB] * SCALE, limit)
                kern = jnp.exp2(kern)
                out[m + k * SUB : m + (k + 1) * SUB, ns] = kern.astype(jnp.bfloat16)
                total += jnp.sum(kern.reshape(SUB // 8, 8, WIDE), axis=0)
        totals.append(jnp.sum(total, axis=0, keepdims=True))
    totals = jnp.concatenate(totals, axis=1)
    for k, (chip, of) in enumerate(PARTS[c]):
        row = pl.ds(block_of(chip, of), 1)
        total = totals[:, k * SUB : (k + 1) * SUB]
        dens_ref[row, :] = total if first else total + dens_ref[row, :]


def basis_of(cols):
    return cols[:, 896:].astype(jnp.float32).T[16:32].astype(jnp.bfloat16)


def pieces(ref, n):
    return [ref.at[pl.ds(k, n)] for k in range(0, ref.shape[0], n)]


def first_tile(pairs_ref, *refs):
    moved, (base_swapped, swapped, k00, dens, basis, rows, cols, sems) = refs[:4], refs[4:]
    swapped = [base_swapped] + pieces(swapped, CHUNK)
    for is_first in (True, False):

        @pl.when((lax.axis_index("core") == 0) == is_first)
        def _(is_first=is_first):
            row_from, col_from = (moved, swapped) if is_first else (swapped, moved)
            plan = [(row_from, rows, c) for c in ROW_COPIES[0][0 if is_first else 1]]
            start_all(plan + [(col_from, cols, c) for c in COL_COPIES[0]], sems)

    dens[...] = jnp.zeros_like(dens)
    block_sums(0, rows, 0, cols, k00, pairs_ref, dens, first=True)
    basis[...] = basis_of(cols)


def second_tile(pairs_ref, *refs):
    moved, swapped, refs = refs[:3], pieces(refs[3], 256), refs[4:]
    rows0, cols0, old, k01, k10, k11, dens, basis, rows, cols, sems = refs
    for is_first in (True, False):

        @pl.when((lax.axis_index("core") == 0) == is_first)
        def _(is_first=is_first):
            row_from, col_from = (moved, swapped) if is_first else (swapped, moved)
            plan = [(row_from, rows, c) for c in ROW_COPIES[1][0 if is_first else 1]]
            start_all(plan + [(col_from, cols, c) for c in COL_COPIES[1]], sems)

    dens[...] = old[...]
    block_sums(0, rows0, 1, cols, k01, pairs_ref, dens, first=True)
    block_sums(1, rows, 0, cols0, k10, pairs_ref, dens)
    block_sums(1, rows, 1, cols, k11, pairs_ref, dens)
    basis[...] = basis_of(cols)


def third_tile(pairs_ref, *refs):
    moved, refs = refs[:3], refs[3:]
    rows0, rows1, cols0, cols1, old, k20, k21, k02, k12, dens, held, sems = refs
    dens[...] = old[...]

    @pl.when(lax.axis_index("core") == 0)
    def _():
        start_all([(moved, held, c) for c in ROW_COPIES[2][0]], sems)
        rows = held.at[pl.ds(0, CHUNK)]
        block_sums(2, rows, 0, cols0, k20, pairs_ref, dens)
        block_sums(2, rows, 1, cols1, k21, pairs_ref, dens)

    @pl.when(lax.axis_index("core") == 1)
    def _():
        start_all([(moved, held, c) for c in COL_COPIES[2]], sems)
        block_sums(0, rows0, 2, held, k02, pairs_ref, dens)
        block_sums(1, rows1, 2, held, k12, pairs_ref, dens)


def fourth_tile(pairs_ref, *refs):
    swapped, refs = pieces(refs[0], 256), refs[1:]
    rows0, rows1, cols0, cols1, held, old, p20, p21, p02, p12 = refs[:10]
    k20, k21, k02, k12, k22, dens, basis, new, copy_sems, sems = refs[10:]
    dens[...] = old[...]

    def keep(*blocks):
        copies = [pltpu.make_async_copy(a, b, copy_sems.at[k]) for k, (a, b) in enumerate(blocks)]
        for c in copies:
            c.start()
        return copies

    @pl.when(lax.axis_index("core") == 0)
    def _():
        copies = keep((p20, k20), (p21, k21))
        start_all([(swapped, new, c) for c in COL_COPIES[2]], sems)
        basis[...] = basis_of(new)
        block_sums(0, rows0, 2, new, k02, pairs_ref, dens)
        block_sums(1, rows1, 2, new, k12, pairs_ref, dens)
        block_sums(2, held.at[pl.ds(0, CHUNK)], 2, new, k22, pairs_ref, dens)
        for c in copies:
            c.wait()

    @pl.when(lax.axis_index("core") == 1)
    def _():
        copies = keep((p02, k02), (p12, k12))
        start_all([(swapped, new, c) for c in ROW_COPIES[2][1]], sems)
        rows = new.at[pl.ds(0, CHUNK)]
        basis[...] = basis_of(held)
        block_sums(2, rows, 0, cols0, k20, pairs_ref, dens)
        block_sums(2, rows, 1, cols1, k21, pairs_ref, dens)
        block_sums(2, rows, 2, held, k22, pairs_ref, dens)
        for c in copies:
            c.wait()


def tile_call(kernel, pairs, operands, blocks, others, scratch=()):
    units = sum(N_ROWS[r] * N_COLS[c] for r, c in blocks)
    result = pl.pallas_call(
        kernel,
        in_specs=[SMEM] + [VMEM] * len(operands),
        out_specs=[VMEM] * (len(blocks) + len(others)),
        out_shape=[jax.ShapeDtypeStruct((N_ROWS[r], N_COLS[c]), jnp.bfloat16) for r, c in blocks]
        + [jax.ShapeDtypeStruct(*o) for o in others],
        scratch_shapes=[*scratch, pltpu.SemaphoreType.DMA((8,))],
        compiler_params=params(12),
        cost_estimate=pl.CostEstimate(flops=units, bytes_accessed=units, transcendentals=0),
        name=kernel.__name__,
    )(pairs, *operands)
    return dict(zip(blocks, result)), *result[len(blocks) :]


def scale_kernel(keys, t0, t1, b0, b1, b2, *refs):
    kern, refs = dict(zip(keys, refs)), refs[len(keys) :]
    there_ref, here_ref, density_ref, inv, s0, s1, s2 = refs
    total = t0[...] + t1[...]
    inv[...] = total
    density_ref[...] = inv[pl.ds(block_of(0, lax.axis_index("core")), 1), :]
    inv[...] = 1.0 / total
    for part, basis, scaled in zip(PARTS, (b0, b1, b2), (s0, s1, s2)):
        inverse = jnp.concatenate([inv[pl.ds(block_of(*s), 1), :] for s in part], axis=1)
        first = lax.broadcasted_iota(jnp.int32, (16, inverse.shape[1]), 0) == 0
        scaled[:16, :] = (basis[...].astype(jnp.float32) * inverse).astype(jnp.bfloat16)
        scaled[16:, :] = jnp.where(first, inverse, 0.0).astype(jnp.bfloat16)
    row_sums(1, (s0, s1, s2), kern, there_ref)
    row_sums(0, (s0, s1, s2), kern, here_ref)


def row_sums(pair, scaled, kern, out_ref):
    for r in range(3):
        at = [k for k, chip in enumerate(ROWS[r]) if CHIPS[chip][1] == pair]
        if not at:
            continue
        ms = slice(at[0] * SUB, (at[-1] + 1) * SUB)
        both = sum(
            lax.dot_general(
                s[...],
                kern[r, c][ms, :],
                (((1,), (1,)), ((), ())),
                preferred_element_type=jnp.float32,
            )
            for c, s in enumerate(scaled)
        )
        for k in at:
            part = both[:24, (k - at[0]) * SUB : (k - at[0] + 1) * SUB]
            out_ref[CHIPS[ROWS[r][k]][0]] = part


def finish(a_ref, b_ref, c_ref, d_ref, out_ref):
    total = a_ref[...] + b_ref[...] + c_ref[...] + d_ref[...]
    out_ref[...] = total[:16] / total[16:17]


def body(coords, basis, pairs):
    f32 = lambda *s: jax.ShapeDtypeStruct(s, jnp.float32)
    form = lambda *s: jax.ShapeDtypeStruct((CHUNK, LANES), jnp.bfloat16)
    own = pl.pallas_call(
        prepare,
        in_specs=[pl.BlockSpec(memory_space=pltpu.HBM)] * 2,
        out_specs=VMEM,
        out_shape=form(),
        scratch_shapes=[
            pltpu.VMEM((SUB, D), jnp.bfloat16),
            pltpu.VMEM((16, SUB), jnp.bfloat16),
            pltpu.SemaphoreType.DMA((2,)),
        ],
        compiler_params=params(8),
        name="prepare",
    )(coords, basis)
    base, base_swapped = pl.pallas_call(
        prepare_other,
        in_specs=[VMEM] * 3,
        out_specs=[VMEM] * 2,
        out_shape=[form(), form()],
        compiler_params=params(8),
        name="prepare_other",
    )(own, swap(coords), swap(basis))
    join = lambda *arrays: jnp.concatenate(arrays)
    sums = ((16, SUB), jnp.float32)
    basis_cols = [((16, n), jnp.bfloat16) for n in N_COLS]
    frames = lambda n: ((n, LANES), jnp.bfloat16)

    over = across(base)
    down = along(base, -1)
    up = along(base, 1)
    swapped = swap(join(up, down, over))
    a3 = across(up[128:])
    a2 = along(down[128:], -1)
    a1 = along(join(up[:128], over[:128]), 1)
    kern, dens, b0, rows0, cols0 = tile_call(
        first_tile,
        pairs,
        (base, up, down, over, base_swapped, swapped),
        ((0, 0),),
        (sums, basis_cols[0], frames(N_ROWS[0]), frames(N_COLS[0])),
    )
    a1, a2, a3, dens, over, down = together(a1, a2, a3, dens, over, down)
    swapped = swap(join(a1, a2, a3))
    z3 = across(join(down[256:], a2[128:]))
    z2 = along(over[:256], -1)
    z1 = along(join(a1[128:], a3[:128]), 1)
    more, dens, b1, rows1, cols1 = tile_call(
        second_tile,
        pairs,
        (a1, a2, a3, swapped, rows0, cols0, dens),
        ((0, 1), (1, 0), (1, 1)),
        (sums, basis_cols[1], frames(N_ROWS[1]), frames(N_COLS[1])),
    )
    kern.update(more)
    dens, z3, z2, z1 = together(dens, z3, z2, z1)
    swapped = swap(join(z1, z2, z3))
    blocks = ((2, 0), (2, 1), (0, 2), (1, 2))
    more, dens, held = tile_call(
        third_tile,
        pairs,
        (z1, z2, z3, rows0, rows1, cols0, cols1, dens),
        blocks,
        (sums, frames(N_COLS[2])),
    )
    more, dens, b2 = tile_call(
        fourth_tile,
        pairs,
        (swapped, rows0, rows1, cols0, cols1, held, dens, *[more[k] for k in blocks]),
        blocks + ((2, 2),),
        (sums, basis_cols[2]),
        [pltpu.VMEM((N_COLS[2], LANES), jnp.bfloat16), pltpu.SemaphoreType.DMA((2,))],
    )
    kern.update(more)

    t = dens + swap(dens)
    t = t + fetch(t, dict(COL_PAIR, core=1))
    t = t + fetch(t, dict(z=lambda z: z ^ 1, core=1))
    keys = tuple(sorted(kern))
    blocks = [kern[k] for k in keys]
    there, here, density = pl.pallas_call(
        functools.partial(scale_kernel, keys),
        in_specs=[VMEM] * 14,
        out_specs=[VMEM] * 3,
        out_shape=[f32(4, 24, SUB), f32(4, 24, SUB), f32(1, SUB)],
        scratch_shapes=[pltpu.VMEM((16, SUB), jnp.float32)]
        + [pltpu.VMEM((32, n), jnp.bfloat16) for n in N_COLS],
        compiler_params=params(12),
        name="scale",
    )(t, fetch(t, dict(z=lambda z: 3 - z, core=1)), b0, b1, b2, *blocks)

    total = swap(here) + fetch(there, dict(ROW_PAIR, core=1))
    diffused = pl.pallas_call(
        finish,
        in_specs=[VMEM] * 4,
        out_specs=VMEM,
        out_shape=f32(16, SUB),
        compiler_params=params(8),
        name="finish",
    )(
        swap(total[0]),
        fetch(total[1], dict(x=-1, core=1)),
        fetch(total[3], dict(x=1, core=1)),
        fetch(total[2], dict(x=2, core=1)),
    )
    return diffused, density.reshape(SUB)


def solution(mesh):
    physical = Mesh(mesh.devices.reshape(SIZES), AXES)
    return jax.shard_map(
        body,
        mesh=physical,
        in_specs=(P(AXES, None), P(None, AXES), P()),
        out_specs=(P(None, AXES), P(AXES)),
        check_vma=False,
    )
```

```python
import functools
import math

import jax
import jax.numpy as jnp
from jax import lax
from jax.experimental import pallas as pl
from jax.experimental.pallas import tpu as pltpu
from jax.sharding import Mesh, PartitionSpec as P

D = 900
LANES = 1024
SUB = 192
CHUNK = 2 * SUB
WIDE = 256
AXES = ("ylo", "z", "core", "x", "yhi")
SIZES = (2, 4, 2, 4, 2)
SCALE = 2.0 * math.log2(math.e) / (0.25 * D)
NEG = -1e30
ROW_PAIR = dict(ylo=1)
COL_PAIR = dict(ylo=1, yhi=1)
CHIPS = ((0, 0), (1, 0), (3, 0), (0, 1), (2, 0), (1, 1), (3, 1), (2, 1))
ROWS = ((0, 1, 2, 3), (4, 5), (6, 7))
PARTS = tuple(tuple((chip, core) for chip in chips for core in (1, 0)) for chips in ROWS)
ROW_COPIES = (
    tuple(tuple((k, core * SUB, k * SUB, SUB) for k in range(4)) for core in (0, 1)),
    (
        ((0, 0, 0, 128), (1, 0, 128, 64), (0, 128, SUB, 128), (2, 0, SUB + 128, 64)),
        ((1, 64, 0, SUB), (2, 64, SUB, SUB)),
    ),
    (
        ((1, 0, 0, SUB), (0, 0, SUB, SUB)),
        ((1, SUB, 0, 64), (2, 0, 64, 128), (0, SUB, SUB, 64), (2, 128, SUB + 64, 128)),
    ),
)
COL_COPIES = (
    tuple((k, 0, k * CHUNK, CHUNK) for k in range(4)),
    ((0, 0, 0, 128), (1, 0, 128, 256), (0, 128, CHUNK, 128), (2, 0, CHUNK + 128, 256)),
    ((1, 0, 0, 256), (2, 0, 256, 128), (0, 0, CHUNK, 256), (2, 128, CHUNK + 256, 128)),
)
N_ROWS = tuple(len(r) * SUB for r in ROWS)
N_COLS = tuple(len(c) * SUB for c in PARTS)
VMEM = pl.BlockSpec(memory_space=pltpu.VMEM)
SMEM = pl.BlockSpec(memory_space=pltpu.SMEM)


def params(mib):
    return pltpu.CompilerParams(vmem_limit_bytes=mib * 2**20)


def fetch(array, first, second=None):
    pairs = []
    for dst in range(math.prod(SIZES)):
        rest, coords = dst, []
        for size in reversed(SIZES):
            coords.append(rest % size)
            rest //= size
        coords.reverse()
        delta = second if second is not None and coords[2] else first
        src = 0
        for axis, size, at in zip(AXES, SIZES, coords):
            by = delta.get(axis, 0)
            src = src * size + (by(at) if callable(by) else (at + by) % size)
        pairs.append((src, dst))
    return lax.ppermute(array, AXES, pairs)


def along(array, by):
    return fetch(array, dict(x=by), dict(z=by))


def across(array):
    return fetch(array, ROW_PAIR, COL_PAIR)


def swap(array):
    return fetch(array, dict(core=1))


def together(*arrays):
    return lax.optimization_barrier(arrays)


def forms(ref, basis_ref):
    lane = lax.broadcasted_iota(jnp.int32, (SUB, 128), 1)
    values = ref[...].astype(jnp.float32)
    sq = -0.5 * jnp.sum(values * values, axis=1, keepdims=True)
    high = sq.astype(jnp.bfloat16).astype(jnp.float32)
    mid = (sq - high).astype(jnp.bfloat16).astype(jnp.float32)
    low = (sq - high - mid).astype(jnp.bfloat16).astype(jnp.float32)
    tail = jnp.concatenate([values[:, 896:], jnp.zeros((SUB, 124), jnp.float32)], axis=1)
    basis = basis_ref[...].astype(jnp.float32)
    basis = jnp.concatenate([jnp.zeros((16, SUB)), basis, jnp.zeros((96, SUB))], axis=0).T

    def fill(first, ones_at, rest):
        out = jnp.where(lane == first, high, rest)
        out = jnp.where(lane == first + 1, mid, out)
        out = jnp.where(lane == first + 2, low, out)
        return jnp.where((lane >= ones_at) & (lane < ones_at + 3), 1.0, out)

    row_form, col_form = fill(4, 7, tail), fill(7, 4, tail + basis)
    is_first = lax.axis_index("core") == 0
    moved = jnp.where(is_first, row_form, col_form).astype(jnp.bfloat16)
    return moved, jnp.where(is_first, col_form, row_form).astype(jnp.bfloat16)


def prepare(coords_hbm, basis_hbm, out_ref, coords_ref, basis_ref, sems):
    copies = [
        pltpu.make_async_copy(coords_hbm, coords_ref, sems.at[0]),
        pltpu.make_async_copy(basis_hbm, basis_ref, sems.at[1]),
    ]
    for c in copies:
        c.start()
    for c in copies:
        c.wait()
    out_ref[:SUB, :896] = coords_ref[:, :896]
    out_ref[SUB:, :896] = coords_ref[:, :896]
    out_ref[:SUB, 896:], out_ref[SUB:, 896:] = forms(coords_ref, basis_ref)


def prepare_other(own_ref, coords_ref, basis_ref, base_ref, swapped_ref):
    base_ref[:SUB], swapped_ref[SUB:] = own_ref[:SUB], own_ref[SUB:]
    base_ref[SUB:, :896] = coords_ref[:, :896]
    swapped_ref[:SUB, :896] = coords_ref[:, :896]
    base_ref[SUB:, 896:], swapped_ref[:SUB, 896:] = forms(coords_ref, basis_ref)


def block_of(chip, core):
    dz, dyl = CHIPS[chip]
    ylo = lax.rem(lax.axis_index("ylo") + dyl, 2)
    return (ylo * 4 + lax.rem(lax.axis_index("z") + dz, 4)) * 2 + core


def start_all(plan, sems):
    copies = [
        pltpu.make_async_copy(src[k].at[pl.ds(at, n)], dst.at[pl.ds(to, n)], sems.at[sem])
        for sem, (src, dst, (k, at, to, n)) in enumerate(plan)
    ]
    for c in copies:
        c.start()
    for c in copies:
        c.wait()


def block_sums(r, rows, c, cols, out, pairs_ref, dens_ref, first=False):
    core = lax.axis_index("core")
    width = N_COLS[c]
    lane = lax.broadcasted_iota(jnp.int32, (1, width), 1)
    limits = {}
    for pair in sorted({CHIPS[k][1] for k in ROWS[r]}):
        limit = jnp.zeros((1, width), jnp.float32)
        for k, (chip, of) in enumerate(PARTS[c]):
            here = (lane >= k * SUB) & (lane < (k + 1) * SUB)
            live = pairs_ref[block_of(3 * pair, core), block_of(chip, of)] > 0
            limit = jnp.where(here, jnp.where(live, 0.0, NEG), limit)
        limits[pair] = limit
    totals = []
    for at in range(0, width, WIDE):
        ns = slice(at, at + WIDE)
        total = jnp.zeros((8, WIDE), jnp.float32)
        for m in range(0, N_ROWS[r], CHUNK):
            gram = lax.dot_general(
                rows[m : m + CHUNK, :],
                cols[ns, :],
                (((1,), (1,)), ((), ())),
                preferred_element_type=jnp.float32,
            )
            for k in range(CHUNK // SUB):
                limit = limits[CHIPS[ROWS[r][m // SUB + k]][1]][:, ns]
                kern = jnp.minimum(gram[k * SUB : (k + 1) * SUB] * SCALE, limit)
                kern = jnp.exp2(kern)
                out[m + k * SUB : m + (k + 1) * SUB, ns] = kern.astype(jnp.bfloat16)
                total += jnp.sum(kern.reshape(SUB // 8, 8, WIDE), axis=0)
        totals.append(jnp.sum(total, axis=0, keepdims=True))
    totals = jnp.concatenate(totals, axis=1)
    for k, (chip, of) in enumerate(PARTS[c]):
        row = pl.ds(block_of(chip, of), 1)
        total = totals[:, k * SUB : (k + 1) * SUB]
        dens_ref[row, :] = total if first else total + dens_ref[row, :]


def basis_of(cols):
    return cols[:, 896:].astype(jnp.float32).T[16:32].astype(jnp.bfloat16)


def pieces(ref, n):
    return [ref.at[pl.ds(k, n)] for k in range(0, ref.shape[0], n)]


def first_tile(pairs_ref, *refs):
    moved, (base_swapped, swapped, k00, dens, basis, rows, cols, sems) = refs[:4], refs[4:]
    swapped = [base_swapped] + pieces(swapped, CHUNK)
    for is_first in (True, False):

        @pl.when((lax.axis_index("core") == 0) == is_first)
        def _(is_first=is_first):
            row_from, col_from = (moved, swapped) if is_first else (swapped, moved)
            plan = [(row_from, rows, c) for c in ROW_COPIES[0][0 if is_first else 1]]
            start_all(plan + [(col_from, cols, c) for c in COL_COPIES[0]], sems)

    dens[...] = jnp.zeros_like(dens)
    block_sums(0, rows, 0, cols, k00, pairs_ref, dens, first=True)
    basis[...] = basis_of(cols)


def second_tile(pairs_ref, *refs):
    moved, swapped, refs = refs[:3], pieces(refs[3], 256), refs[4:]
    rows0, cols0, old, k01, k10, k11, dens, basis, rows, cols, sems = refs
    for is_first in (True, False):

        @pl.when((lax.axis_index("core") == 0) == is_first)
        def _(is_first=is_first):
            row_from, col_from = (moved, swapped) if is_first else (swapped, moved)
            plan = [(row_from, rows, c) for c in ROW_COPIES[1][0 if is_first else 1]]
            start_all(plan + [(col_from, cols, c) for c in COL_COPIES[1]], sems)

    dens[...] = old[...]
    block_sums(0, rows0, 1, cols, k01, pairs_ref, dens, first=True)
    block_sums(1, rows, 0, cols0, k10, pairs_ref, dens)
    block_sums(1, rows, 1, cols, k11, pairs_ref, dens)
    basis[...] = basis_of(cols)


def third_tile(pairs_ref, *refs):
    moved, refs = refs[:3], refs[3:]
    rows0, rows1, cols0, cols1, old, k20, k21, k02, k12, dens, held, sems = refs
    dens[...] = old[...]

    @pl.when(lax.axis_index("core") == 0)
    def _():
        start_all([(moved, held, c) for c in ROW_COPIES[2][0]], sems)
        rows = held.at[pl.ds(0, CHUNK)]
        block_sums(2, rows, 0, cols0, k20, pairs_ref, dens)
        block_sums(2, rows, 1, cols1, k21, pairs_ref, dens)

    @pl.when(lax.axis_index("core") == 1)
    def _():
        start_all([(moved, held, c) for c in COL_COPIES[2]], sems)
        block_sums(0, rows0, 2, held, k02, pairs_ref, dens)
        block_sums(1, rows1, 2, held, k12, pairs_ref, dens)


def fourth_tile(pairs_ref, *refs):
    swapped, refs = pieces(refs[0], 256), refs[1:]
    rows0, rows1, cols0, cols1, held, old, p20, p21, p02, p12 = refs[:10]
    k20, k21, k02, k12, k22, dens, basis, new, copy_sems, sems = refs[10:]
    dens[...] = old[...]

    def keep(*blocks):
        copies = [pltpu.make_async_copy(a, b, copy_sems.at[k]) for k, (a, b) in enumerate(blocks)]
        for c in copies:
            c.start()
        return copies

    @pl.when(lax.axis_index("core") == 0)
    def _():
        copies = keep((p20, k20), (p21, k21))
        start_all([(swapped, new, c) for c in COL_COPIES[2]], sems)
        basis[...] = basis_of(new)
        block_sums(0, rows0, 2, new, k02, pairs_ref, dens)
        block_sums(1, rows1, 2, new, k12, pairs_ref, dens)
        block_sums(2, held.at[pl.ds(0, CHUNK)], 2, new, k22, pairs_ref, dens)
        for c in copies:
            c.wait()

    @pl.when(lax.axis_index("core") == 1)
    def _():
        copies = keep((p02, k02), (p12, k12))
        start_all([(swapped, new, c) for c in ROW_COPIES[2][1]], sems)
        rows = new.at[pl.ds(0, CHUNK)]
        basis[...] = basis_of(held)
        block_sums(2, rows, 0, cols0, k20, pairs_ref, dens)
        block_sums(2, rows, 1, cols1, k21, pairs_ref, dens)
        block_sums(2, rows, 2, held, k22, pairs_ref, dens)
        for c in copies:
            c.wait()


def tile_call(kernel, pairs, operands, blocks, others, scratch=()):
    units = sum(N_ROWS[r] * N_COLS[c] for r, c in blocks)
    result = pl.pallas_call(
        kernel,
        in_specs=[SMEM] + [VMEM] * len(operands),
        out_specs=[VMEM] * (len(blocks) + len(others)),
        out_shape=[jax.ShapeDtypeStruct((N_ROWS[r], N_COLS[c]), jnp.bfloat16) for r, c in blocks]
        + [jax.ShapeDtypeStruct(*o) for o in others],
        scratch_shapes=[*scratch, pltpu.SemaphoreType.DMA((8,))],
        compiler_params=params(12),
        cost_estimate=pl.CostEstimate(flops=units, bytes_accessed=units, transcendentals=0),
        name=kernel.__name__,
    )(pairs, *operands)
    return dict(zip(blocks, result)), *result[len(blocks) :]


def scale_kernel(keys, t0, t1, b0, b1, b2, *refs):
    kern, refs = dict(zip(keys, refs)), refs[len(keys) :]
    there_ref, density_ref, s0, s1, s2, inv = refs
    total = t0[...] + t1[...]
    inv[...] = total
    density_ref[...] = inv[pl.ds(block_of(0, lax.axis_index("core")), 1), :]
    inv[...] = 1.0 / total
    for part, basis, scaled in zip(PARTS, (b0, b1, b2), (s0, s1, s2)):
        inverse = jnp.concatenate([inv[pl.ds(block_of(*s), 1), :] for s in part], axis=1)
        first = lax.broadcasted_iota(jnp.int32, (16, inverse.shape[1]), 0) == 0
        scaled[:16, :] = (basis[...].astype(jnp.float32) * inverse).astype(jnp.bfloat16)
        scaled[16:, :] = jnp.where(first, inverse, 0.0).astype(jnp.bfloat16)
    row_sums(1, (s0, s1, s2), kern, there_ref)


def here_kernel(keys, s0, s1, s2, *refs):
    row_sums(0, (s0, s1, s2), dict(zip(keys, refs)), refs[len(keys)])


def row_sums(pair, scaled, kern, out_ref):
    for r in range(3):
        at = [k for k, chip in enumerate(ROWS[r]) if CHIPS[chip][1] == pair]
        if not at:
            continue
        ms = slice(at[0] * SUB, (at[-1] + 1) * SUB)
        both = sum(
            lax.dot_general(
                s[...],
                kern[r, c][ms, :],
                (((1,), (1,)), ((), ())),
                preferred_element_type=jnp.float32,
            )
            for c, s in enumerate(scaled)
        )
        for k in at:
            part = both[:24, (k - at[0]) * SUB : (k - at[0] + 1) * SUB]
            out_ref[CHIPS[ROWS[r][k]][0]] = part


def finish(a_ref, b_ref, c_ref, d_ref, out_ref):
    total = a_ref[...] + b_ref[...] + c_ref[...] + d_ref[...]
    out_ref[...] = total[:16] / total[16:17]


def body(coords, basis, pairs):
    f32 = lambda *s: jax.ShapeDtypeStruct(s, jnp.float32)
    form = lambda *s: jax.ShapeDtypeStruct((CHUNK, LANES), jnp.bfloat16)
    own = pl.pallas_call(
        prepare,
        in_specs=[pl.BlockSpec(memory_space=pltpu.HBM)] * 2,
        out_specs=VMEM,
        out_shape=form(),
        scratch_shapes=[
            pltpu.VMEM((SUB, D), jnp.bfloat16),
            pltpu.VMEM((16, SUB), jnp.bfloat16),
            pltpu.SemaphoreType.DMA((2,)),
        ],
        compiler_params=params(8),
        name="prepare",
    )(coords, basis)
    base, base_swapped = pl.pallas_call(
        prepare_other,
        in_specs=[VMEM] * 3,
        out_specs=[VMEM] * 2,
        out_shape=[form(), form()],
        compiler_params=params(8),
        name="prepare_other",
    )(own, swap(coords), swap(basis))
    join = lambda *arrays: jnp.concatenate(arrays)
    sums = ((16, SUB), jnp.float32)
    basis_cols = [((16, n), jnp.bfloat16) for n in N_COLS]
    frames = lambda n: ((n, LANES), jnp.bfloat16)

    over = across(base)
    down = along(base, -1)
    up = along(base, 1)
    swapped = swap(join(up, down, over))
    a3 = across(up[128:])
    a2 = along(down[128:], -1)
    a1 = along(join(up[:128], over[:128]), 1)
    kern, dens, b0, rows0, cols0 = tile_call(
        first_tile,
        pairs,
        (base, up, down, over, base_swapped, swapped),
        ((0, 0),),
        (sums, basis_cols[0], frames(N_ROWS[0]), frames(N_COLS[0])),
    )
    a1, a2, a3, dens, over, down = together(a1, a2, a3, dens, over, down)
    swapped = swap(join(a1, a2, a3))
    z3 = across(join(down[256:], a2[128:]))
    z2 = along(over[:256], -1)
    z1 = along(join(a1[128:], a3[:128]), 1)
    more, dens, b1, rows1, cols1 = tile_call(
        second_tile,
        pairs,
        (a1, a2, a3, swapped, rows0, cols0, dens),
        ((0, 1), (1, 0), (1, 1)),
        (sums, basis_cols[1], frames(N_ROWS[1]), frames(N_COLS[1])),
    )
    kern.update(more)
    dens, z3, z2, z1 = together(dens, z3, z2, z1)
    swapped = swap(join(z1, z2, z3))
    blocks = ((2, 0), (2, 1), (0, 2), (1, 2))
    more, dens, held = tile_call(
        third_tile,
        pairs,
        (z1, z2, z3, rows0, rows1, cols0, cols1, dens),
        blocks,
        (sums, frames(N_COLS[2])),
    )
    more, dens, b2 = tile_call(
        fourth_tile,
        pairs,
        (swapped, rows0, rows1, cols0, cols1, held, dens, *[more[k] for k in blocks]),
        blocks + ((2, 2),),
        (sums, basis_cols[2]),
        [pltpu.VMEM((N_COLS[2], LANES), jnp.bfloat16), pltpu.SemaphoreType.DMA((2,))],
    )
    kern.update(more)

    t = dens + swap(dens)
    t = t + fetch(t, dict(COL_PAIR, core=1))
    t = t + fetch(t, dict(z=lambda z: z ^ 1, core=1))
    keys = tuple(sorted(kern))
    blocks = [kern[k] for k in keys]
    there, density, *scaled = pl.pallas_call(
        functools.partial(scale_kernel, keys),
        in_specs=[VMEM] * 14,
        out_specs=[VMEM] * 5,
        out_shape=[f32(4, 24, SUB), f32(1, SUB)]
        + [jax.ShapeDtypeStruct((32, n), jnp.bfloat16) for n in N_COLS],
        scratch_shapes=[pltpu.VMEM((16, SUB), jnp.float32)],
        compiler_params=params(12),
        name="scale",
    )(t, fetch(t, dict(z=lambda z: 3 - z, core=1)), b0, b1, b2, *blocks)
    here = pl.pallas_call(
        functools.partial(here_kernel, keys),
        in_specs=[VMEM] * 12,
        out_specs=VMEM,
        out_shape=f32(4, 24, SUB),
        compiler_params=params(12),
        name="here",
    )(*scaled, *blocks)

    total = here + fetch(there, ROW_PAIR)
    diffused = pl.pallas_call(
        finish,
        in_specs=[VMEM] * 4,
        out_specs=VMEM,
        out_shape=f32(16, SUB),
        compiler_params=params(8),
        name="finish",
    )(
        total[0],
        fetch(total[1], dict(x=-1)),
        fetch(total[3], dict(x=1)),
        fetch(total[2], dict(x=2)),
    )
    return diffused, density.reshape(SUB)


def solution(mesh):
    physical = Mesh(mesh.devices.reshape(SIZES), AXES)
    return jax.shard_map(
        body,
        mesh=physical,
        in_specs=(P(AXES, None), P(None, AXES), P()),
        out_specs=(P(None, AXES), P(AXES)),
        check_vma=False,
    )
```

```python
import functools
import math

import jax
import jax.numpy as jnp
from jax import lax
from jax.experimental import pallas as pl
from jax.experimental.pallas import tpu as pltpu
from jax.sharding import Mesh, PartitionSpec as P

D = 900
LANES = 1024
SUB = 192
CHUNK = 2 * SUB
WIDE = 256
AXES = ("ylo", "z", "core", "x", "yhi")
SIZES = (2, 4, 2, 4, 2)
SCALE = 2.0 * math.log2(math.e) / (0.25 * D)
NEG = -1e30
ROW_PAIR = dict(ylo=1)
COL_PAIR = dict(ylo=1, yhi=1)
CHIPS = ((0, 0), (1, 0), (3, 0), (0, 1), (2, 0), (1, 1), (3, 1), (2, 1))
ROWS = ((0, 1, 2, 3), (4, 5), (6, 7))
PARTS = tuple(tuple((chip, core) for chip in chips for core in (1, 0)) for chips in ROWS)
ROW_COPIES = (
    tuple(tuple((k, core * SUB, k * SUB, SUB) for k in range(4)) for core in (0, 1)),
    (
        ((0, 0, 0, 128), (1, 0, 128, 64), (0, 128, SUB, 128), (2, 0, SUB + 128, 64)),
        ((1, 64, 0, SUB), (2, 64, SUB, SUB)),
    ),
    (
        ((1, 0, 0, SUB), (0, 0, SUB, SUB)),
        ((1, SUB, 0, 64), (2, 0, 64, 128), (0, SUB, SUB, 64), (2, 128, SUB + 64, 128)),
    ),
)
COL_COPIES = (
    tuple((k, 0, k * CHUNK, CHUNK) for k in range(4)),
    ((0, 0, 0, 128), (1, 0, 128, 256), (0, 128, CHUNK, 128), (2, 0, CHUNK + 128, 256)),
    ((1, 0, 0, 256), (2, 0, 256, 128), (0, 0, CHUNK, 256), (2, 128, CHUNK + 256, 128)),
)
N_ROWS = tuple(len(r) * SUB for r in ROWS)
N_COLS = tuple(len(c) * SUB for c in PARTS)
VMEM = pl.BlockSpec(memory_space=pltpu.VMEM)
SMEM = pl.BlockSpec(memory_space=pltpu.SMEM)


def params(mib):
    return pltpu.CompilerParams(vmem_limit_bytes=mib * 2**20)


def fetch(array, first, second=None):
    pairs = []
    for dst in range(math.prod(SIZES)):
        rest, coords = dst, []
        for size in reversed(SIZES):
            coords.append(rest % size)
            rest //= size
        coords.reverse()
        delta = second if second is not None and coords[2] else first
        src = 0
        for axis, size, at in zip(AXES, SIZES, coords):
            by = delta.get(axis, 0)
            src = src * size + (by(at) if callable(by) else (at + by) % size)
        pairs.append((src, dst))
    return lax.ppermute(array, AXES, pairs)


def along(array, by):
    return fetch(array, dict(x=by), dict(z=by))


def across(array):
    return fetch(array, ROW_PAIR, COL_PAIR)


def swap(array):
    return fetch(array, dict(core=1))


def together(*arrays):
    return lax.optimization_barrier(arrays)


def forms(ref, basis_ref):
    lane = lax.broadcasted_iota(jnp.int32, (SUB, 128), 1)
    values = ref[...].astype(jnp.float32)
    sq = -0.5 * jnp.sum(values * values, axis=1, keepdims=True)
    high = sq.astype(jnp.bfloat16).astype(jnp.float32)
    mid = (sq - high).astype(jnp.bfloat16).astype(jnp.float32)
    low = (sq - high - mid).astype(jnp.bfloat16).astype(jnp.float32)
    tail = jnp.concatenate([values[:, 896:], jnp.zeros((SUB, 124), jnp.float32)], axis=1)
    basis = basis_ref[...].astype(jnp.float32)
    basis = jnp.concatenate([jnp.zeros((16, SUB)), basis, jnp.zeros((96, SUB))], axis=0).T

    def fill(first, ones_at, rest):
        out = jnp.where(lane == first, high, rest)
        out = jnp.where(lane == first + 1, mid, out)
        out = jnp.where(lane == first + 2, low, out)
        return jnp.where((lane >= ones_at) & (lane < ones_at + 3), 1.0, out)

    row_form, col_form = fill(4, 7, tail), fill(7, 4, tail + basis)
    is_first = lax.axis_index("core") == 0
    moved = jnp.where(is_first, row_form, col_form).astype(jnp.bfloat16)
    return moved, jnp.where(is_first, col_form, row_form).astype(jnp.bfloat16)


def prepare(coords_hbm, basis_hbm, out_ref, coords_ref, basis_ref, sems):
    copies = [
        pltpu.make_async_copy(coords_hbm, coords_ref, sems.at[0]),
        pltpu.make_async_copy(basis_hbm, basis_ref, sems.at[1]),
    ]
    for c in copies:
        c.start()
    for c in copies:
        c.wait()
    out_ref[:SUB, :896] = coords_ref[:, :896]
    out_ref[SUB:, :896] = coords_ref[:, :896]
    out_ref[:SUB, 896:], out_ref[SUB:, 896:] = forms(coords_ref, basis_ref)


def prepare_other(own_ref, coords_ref, basis_ref, base_ref, swapped_ref):
    base_ref[:SUB], swapped_ref[SUB:] = own_ref[:SUB], own_ref[SUB:]
    base_ref[SUB:, :896] = coords_ref[:, :896]
    swapped_ref[:SUB, :896] = coords_ref[:, :896]
    base_ref[SUB:, 896:], swapped_ref[:SUB, 896:] = forms(coords_ref, basis_ref)


def block_of(chip, core):
    dz, dyl = CHIPS[chip]
    ylo = lax.rem(lax.axis_index("ylo") + dyl, 2)
    return (ylo * 4 + lax.rem(lax.axis_index("z") + dz, 4)) * 2 + core


def start_all(plan, sems):
    copies = [
        pltpu.make_async_copy(src[k].at[pl.ds(at, n)], dst.at[pl.ds(to, n)], sems.at[sem])
        for sem, (src, dst, (k, at, to, n)) in enumerate(plan)
    ]
    for c in copies:
        c.start()
    for c in copies:
        c.wait()


def block_sums(r, rows, c, cols, out, pairs_ref, dens_ref, first=False):
    core = lax.axis_index("core")
    width = N_COLS[c]
    lane = lax.broadcasted_iota(jnp.int32, (1, width), 1)
    limits = {}
    for pair in sorted({CHIPS[k][1] for k in ROWS[r]}):
        limit = jnp.zeros((1, width), jnp.float32)
        for k, (chip, of) in enumerate(PARTS[c]):
            here = (lane >= k * SUB) & (lane < (k + 1) * SUB)
            live = pairs_ref[block_of(3 * pair, core), block_of(chip, of)] > 0
            limit = jnp.where(here, jnp.where(live, 0.0, NEG), limit)
        limits[pair] = limit
    totals = []
    for at in range(0, width, WIDE):
        ns = slice(at, at + WIDE)
        total = jnp.zeros((8, WIDE), jnp.float32)
        for m in range(0, N_ROWS[r], CHUNK):
            gram = lax.dot_general(
                rows[m : m + CHUNK, :],
                cols[ns, :],
                (((1,), (1,)), ((), ())),
                preferred_element_type=jnp.float32,
            )
            for k in range(CHUNK // SUB):
                limit = limits[CHIPS[ROWS[r][m // SUB + k]][1]][:, ns]
                kern = jnp.minimum(gram[k * SUB : (k + 1) * SUB] * SCALE, limit)
                kern = jnp.exp2(kern)
                out[m + k * SUB : m + (k + 1) * SUB, ns] = kern.astype(jnp.bfloat16)
                total += jnp.sum(kern.reshape(SUB // 8, 8, WIDE), axis=0)
        totals.append(jnp.sum(total, axis=0, keepdims=True))
    totals = jnp.concatenate(totals, axis=1)
    for k, (chip, of) in enumerate(PARTS[c]):
        row = pl.ds(block_of(chip, of), 1)
        total = totals[:, k * SUB : (k + 1) * SUB]
        dens_ref[row, :] = total if first else total + dens_ref[row, :]


def basis_of(cols):
    return cols[:, 896:].astype(jnp.float32).T[16:32].astype(jnp.bfloat16)


def pieces(ref, n):
    return [ref.at[pl.ds(k, n)] for k in range(0, ref.shape[0], n)]


def first_tile(pairs_ref, *refs):
    moved, (base_swapped, swapped, k00, dens, basis, rows, cols, sems) = refs[:4], refs[4:]
    swapped = [base_swapped] + pieces(swapped, CHUNK)
    for is_first in (True, False):

        @pl.when((lax.axis_index("core") == 0) == is_first)
        def _(is_first=is_first):
            row_from, col_from = (moved, swapped) if is_first else (swapped, moved)
            plan = [(row_from, rows, c) for c in ROW_COPIES[0][0 if is_first else 1]]
            start_all(plan + [(col_from, cols, c) for c in COL_COPIES[0]], sems)

    dens[...] = jnp.zeros_like(dens)
    block_sums(0, rows, 0, cols, k00, pairs_ref, dens, first=True)
    basis[...] = basis_of(cols)


def second_tile(pairs_ref, *refs):
    moved, swapped, refs = refs[:3], pieces(refs[3], 256), refs[4:]
    rows0, cols0, old, k01, k10, k11, dens, basis, rows, cols, sems = refs
    for is_first in (True, False):

        @pl.when((lax.axis_index("core") == 0) == is_first)
        def _(is_first=is_first):
            row_from, col_from = (moved, swapped) if is_first else (swapped, moved)
            plan = [(row_from, rows, c) for c in ROW_COPIES[1][0 if is_first else 1]]
            start_all(plan + [(col_from, cols, c) for c in COL_COPIES[1]], sems)

    dens[...] = old[...]
    block_sums(0, rows0, 1, cols, k01, pairs_ref, dens, first=True)
    block_sums(1, rows, 0, cols0, k10, pairs_ref, dens)
    block_sums(1, rows, 1, cols, k11, pairs_ref, dens)
    basis[...] = basis_of(cols)


def third_tile(pairs_ref, *refs):
    moved, refs = refs[:3], refs[3:]
    rows0, rows1, cols0, cols1, old, k20, k21, k02, k12, dens, held, sems = refs
    dens[...] = old[...]

    @pl.when(lax.axis_index("core") == 0)
    def _():
        start_all([(moved, held, c) for c in ROW_COPIES[2][0]], sems)
        rows = held.at[pl.ds(0, CHUNK)]
        block_sums(2, rows, 0, cols0, k20, pairs_ref, dens)
        block_sums(2, rows, 1, cols1, k21, pairs_ref, dens)

    @pl.when(lax.axis_index("core") == 1)
    def _():
        start_all([(moved, held, c) for c in COL_COPIES[2]], sems)
        block_sums(0, rows0, 2, held, k02, pairs_ref, dens)
        block_sums(1, rows1, 2, held, k12, pairs_ref, dens)


def fourth_tile(pairs_ref, *refs):
    swapped, refs = pieces(refs[0], 256), refs[1:]
    rows0, rows1, cols0, cols1, held, old, p20, p21, p02, p12 = refs[:10]
    k20, k21, k02, k12, k22, dens, basis, new, copy_sems, sems = refs[10:]
    dens[...] = old[...]

    def keep(*blocks):
        copies = [pltpu.make_async_copy(a, b, copy_sems.at[k]) for k, (a, b) in enumerate(blocks)]
        for c in copies:
            c.start()
        return copies

    @pl.when(lax.axis_index("core") == 0)
    def _():
        copies = keep((p20, k20), (p21, k21))
        start_all([(swapped, new, c) for c in COL_COPIES[2]], sems)
        basis[...] = basis_of(new)
        block_sums(0, rows0, 2, new, k02, pairs_ref, dens)
        block_sums(1, rows1, 2, new, k12, pairs_ref, dens)
        block_sums(2, held.at[pl.ds(0, CHUNK)], 2, new, k22, pairs_ref, dens)
        for c in copies:
            c.wait()

    @pl.when(lax.axis_index("core") == 1)
    def _():
        copies = keep((p02, k02), (p12, k12))
        start_all([(swapped, new, c) for c in ROW_COPIES[2][1]], sems)
        rows = new.at[pl.ds(0, CHUNK)]
        basis[...] = basis_of(held)
        block_sums(2, rows, 0, cols0, k20, pairs_ref, dens)
        block_sums(2, rows, 1, cols1, k21, pairs_ref, dens)
        block_sums(2, rows, 2, held, k22, pairs_ref, dens)
        for c in copies:
            c.wait()


def tile_call(kernel, pairs, operands, blocks, others, scratch=()):
    units = sum(N_ROWS[r] * N_COLS[c] for r, c in blocks)
    result = pl.pallas_call(
        kernel,
        in_specs=[SMEM] + [VMEM] * len(operands),
        out_specs=[VMEM] * (len(blocks) + len(others)),
        out_shape=[jax.ShapeDtypeStruct((N_ROWS[r], N_COLS[c]), jnp.bfloat16) for r, c in blocks]
        + [jax.ShapeDtypeStruct(*o) for o in others],
        scratch_shapes=[*scratch, pltpu.SemaphoreType.DMA((8,))],
        compiler_params=params(12),
        cost_estimate=pl.CostEstimate(flops=units, bytes_accessed=units, transcendentals=0),
        name=kernel.__name__,
    )(pairs, *operands)
    return dict(zip(blocks, result)), *result[len(blocks) :]


def scale_kernel(keys, t0, t1, b0, b1, b2, *refs):
    kern, refs = dict(zip(keys, refs)), refs[len(keys) :]
    there_ref, density_ref, s0, s1, s2, inv = refs
    total = t0[...] + t1[...]
    inv[...] = total
    density_ref[...] = inv[pl.ds(block_of(0, lax.axis_index("core")), 1), :]
    inv[...] = 1.0 / total
    for part, basis, scaled in zip(PARTS, (b0, b1, b2), (s0, s1, s2)):
        inverse = jnp.concatenate([inv[pl.ds(block_of(*s), 1), :] for s in part], axis=1)
        first = lax.broadcasted_iota(jnp.int32, (16, inverse.shape[1]), 0) == 0
        scaled[:16, :] = (basis[...].astype(jnp.float32) * inverse).astype(jnp.bfloat16)
        scaled[16:, :] = jnp.where(first, inverse, 0.0).astype(jnp.bfloat16)
    row_sums(1, (s0, s1, s2), kern, there_ref)


def here_kernel(keys, s0, s1, s2, *refs):
    row_sums(0, (s0, s1, s2), dict(zip(keys, refs)), refs[len(keys)])


def row_sums(pair, scaled, kern, out_ref):
    for r in range(3):
        at = [k for k, chip in enumerate(ROWS[r]) if CHIPS[chip][1] == pair]
        if not at:
            continue
        ms = slice(at[0] * SUB, (at[-1] + 1) * SUB)
        both = sum(
            lax.dot_general(
                s[...],
                kern[r, c][ms, :],
                (((1,), (1,)), ((), ())),
                preferred_element_type=jnp.float32,
            )
            for c, s in enumerate(scaled)
        )
        for k in at:
            part = both[:24, (k - at[0]) * SUB : (k - at[0] + 1) * SUB]
            dx = CHIPS[ROWS[r][k]][0]
            out_ref[dx * 16 : (dx + 1) * 16] = part[:16]
            out_ref[64 + dx : 65 + dx] = part[16:17]


def finish(a_ref, b_ref, c_ref, d_ref, out_ref):
    total = a_ref[...] + b_ref[...] + c_ref[...] + d_ref[...]
    out_ref[...] = total[:16] / total[16:17]


def body(coords, basis, pairs):
    f32 = lambda *s: jax.ShapeDtypeStruct(s, jnp.float32)
    form = lambda *s: jax.ShapeDtypeStruct((CHUNK, LANES), jnp.bfloat16)
    own = pl.pallas_call(
        prepare,
        in_specs=[pl.BlockSpec(memory_space=pltpu.HBM)] * 2,
        out_specs=VMEM,
        out_shape=form(),
        scratch_shapes=[
            pltpu.VMEM((SUB, D), jnp.bfloat16),
            pltpu.VMEM((16, SUB), jnp.bfloat16),
            pltpu.SemaphoreType.DMA((2,)),
        ],
        compiler_params=params(8),
        name="prepare",
    )(coords, basis)
    base, base_swapped = pl.pallas_call(
        prepare_other,
        in_specs=[VMEM] * 3,
        out_specs=[VMEM] * 2,
        out_shape=[form(), form()],
        compiler_params=params(8),
        name="prepare_other",
    )(own, swap(coords), swap(basis))
    join = lambda *arrays: jnp.concatenate(arrays)
    sums = ((16, SUB), jnp.float32)
    basis_cols = [((16, n), jnp.bfloat16) for n in N_COLS]
    frames = lambda n: ((n, LANES), jnp.bfloat16)

    over = across(base)
    down = along(base, -1)
    up = along(base, 1)
    swapped = swap(join(up, down, over))
    a3 = across(up[128:])
    a2 = along(down[128:], -1)
    a1 = along(join(up[:128], over[:128]), 1)
    kern, dens, b0, rows0, cols0 = tile_call(
        first_tile,
        pairs,
        (base, up, down, over, base_swapped, swapped),
        ((0, 0),),
        (sums, basis_cols[0], frames(N_ROWS[0]), frames(N_COLS[0])),
    )
    a1, a2, a3, dens, over, down = together(a1, a2, a3, dens, over, down)
    swapped = swap(join(a1, a2, a3))
    z3 = across(join(down[256:], a2[128:]))
    z2 = along(over[:256], -1)
    z1 = along(join(a1[128:], a3[:128]), 1)
    more, dens, b1, rows1, cols1 = tile_call(
        second_tile,
        pairs,
        (a1, a2, a3, swapped, rows0, cols0, dens),
        ((0, 1), (1, 0), (1, 1)),
        (sums, basis_cols[1], frames(N_ROWS[1]), frames(N_COLS[1])),
    )
    kern.update(more)
    dens, z3, z2, z1 = together(dens, z3, z2, z1)
    swapped = swap(join(z1, z2, z3))
    blocks = ((2, 0), (2, 1), (0, 2), (1, 2))
    more, dens, held = tile_call(
        third_tile,
        pairs,
        (z1, z2, z3, rows0, rows1, cols0, cols1, dens),
        blocks,
        (sums, frames(N_COLS[2])),
    )
    more, dens, b2 = tile_call(
        fourth_tile,
        pairs,
        (swapped, rows0, rows1, cols0, cols1, held, dens, *[more[k] for k in blocks]),
        blocks + ((2, 2),),
        (sums, basis_cols[2]),
        [pltpu.VMEM((N_COLS[2], LANES), jnp.bfloat16), pltpu.SemaphoreType.DMA((2,))],
    )
    kern.update(more)

    t = dens + swap(dens)
    t = t + fetch(t, dict(COL_PAIR, core=1))
    t = t + fetch(t, dict(z=lambda z: 3 - z, core=1))
    keys = tuple(sorted(kern))
    blocks = [kern[k] for k in keys]
    there, density, *scaled = pl.pallas_call(
        functools.partial(scale_kernel, keys),
        in_specs=[VMEM] * 14,
        out_specs=[VMEM] * 5,
        out_shape=[f32(72, SUB), f32(1, SUB)]
        + [jax.ShapeDtypeStruct((32, n), jnp.bfloat16) for n in N_COLS],
        scratch_shapes=[pltpu.VMEM((16, SUB), jnp.float32)],
        compiler_params=params(12),
        name="scale",
    )(t, fetch(t, dict(z=lambda z: z ^ 1, core=1)), b0, b1, b2, *blocks)
    here = pl.pallas_call(
        functools.partial(here_kernel, keys),
        in_specs=[VMEM] * 12,
        out_specs=VMEM,
        out_shape=f32(72, SUB),
        compiler_params=params(12),
        name="here",
    )(*scaled, *blocks)

    total = here + fetch(there, ROW_PAIR)
    shard = lambda k: jnp.concatenate([total[16 * k : 16 * k + 16], total[64 + k : 65 + k]])
    diffused = pl.pallas_call(
        finish,
        in_specs=[VMEM] * 4,
        out_specs=VMEM,
        out_shape=f32(16, SUB),
        compiler_params=params(8),
        name="finish",
    )(
        shard(0),
        fetch(shard(2), dict(x=2)),
        fetch(shard(1), dict(x=-1)),
        fetch(shard(3), dict(x=1)),
    )
    return diffused, density.reshape(SUB)


def solution(mesh):
    physical = Mesh(mesh.devices.reshape(SIZES), AXES)
    return jax.shard_map(
        body,
        mesh=physical,
        in_specs=(P(AXES, None), P(None, AXES), P()),
        out_specs=(P(None, AXES), P(AXES)),
        check_vma=False,
    )
```

```python
import functools
import math

import jax
import jax.numpy as jnp
from jax import lax
from jax.experimental import pallas as pl
from jax.experimental.pallas import tpu as pltpu
from jax.sharding import Mesh, PartitionSpec as P

D = 900
LANES = 1024
SUB = 192
CHUNK = 2 * SUB
WIDE = 256
AXES = ("ylo", "z", "core", "x", "yhi")
SIZES = (2, 4, 2, 4, 2)
SCALE = 2.0 * math.log2(math.e) / (0.25 * D)
NEG = -1e30
ROW_PAIR = dict(ylo=1)
COL_PAIR = dict(ylo=1, yhi=1)
CHIPS = ((0, 0), (1, 0), (3, 0), (0, 1), (2, 0), (1, 1), (3, 1), (2, 1))
ROWS = ((0, 1, 2, 3), (4, 5), (6, 7))
PARTS = tuple(tuple((chip, core) for chip in chips for core in (1, 0)) for chips in ROWS)
ROW_COPIES = (
    tuple(tuple((k, core * SUB, k * SUB, SUB) for k in range(4)) for core in (0, 1)),
    (
        ((0, 0, 0, 128), (1, 0, 128, 64), (0, 128, SUB, 128), (2, 0, SUB + 128, 64)),
        ((1, 64, 0, SUB), (2, 64, SUB, SUB)),
    ),
    (
        ((1, 0, 0, SUB), (0, 0, SUB, SUB)),
        ((1, SUB, 0, 64), (2, 0, 64, 128), (0, SUB, SUB, 64), (2, 128, SUB + 64, 128)),
    ),
)
COL_COPIES = (
    tuple((k, 0, k * CHUNK, CHUNK) for k in range(4)),
    ((0, 0, 0, 128), (1, 0, 128, 256), (0, 128, CHUNK, 128), (2, 0, CHUNK + 128, 256)),
    ((1, 0, 0, 256), (2, 0, 256, 128), (0, 0, CHUNK, 256), (2, 128, CHUNK + 256, 128)),
)
N_ROWS = tuple(len(r) * SUB for r in ROWS)
N_COLS = tuple(len(c) * SUB for c in PARTS)
VMEM = pl.BlockSpec(memory_space=pltpu.VMEM)
SMEM = pl.BlockSpec(memory_space=pltpu.SMEM)


def params(mib):
    return pltpu.CompilerParams(vmem_limit_bytes=mib * 2**20)


def fetch(array, first, second=None):
    pairs = []
    for dst in range(math.prod(SIZES)):
        rest, coords = dst, []
        for size in reversed(SIZES):
            coords.append(rest % size)
            rest //= size
        coords.reverse()
        delta = second if second is not None and coords[2] else first
        src = 0
        for axis, size, at in zip(AXES, SIZES, coords):
            by = delta.get(axis, 0)
            src = src * size + (by(at) if callable(by) else (at + by) % size)
        pairs.append((src, dst))
    return lax.ppermute(array, AXES, pairs)


def along(array, by):
    return fetch(array, dict(x=by), dict(z=by))


def across(array):
    return fetch(array, ROW_PAIR, COL_PAIR)


def swap(array):
    return fetch(array, dict(core=1))


def together(*arrays):
    return lax.optimization_barrier(arrays)


def forms(ref, basis_ref):
    lane = lax.broadcasted_iota(jnp.int32, (SUB, 128), 1)
    values = ref[...].astype(jnp.float32)
    sq = -0.5 * jnp.sum(values * values, axis=1, keepdims=True)
    high = sq.astype(jnp.bfloat16).astype(jnp.float32)
    mid = (sq - high).astype(jnp.bfloat16).astype(jnp.float32)
    low = (sq - high - mid).astype(jnp.bfloat16).astype(jnp.float32)
    tail = jnp.concatenate([values[:, 896:], jnp.zeros((SUB, 124), jnp.float32)], axis=1)
    basis = basis_ref[...].astype(jnp.float32)
    basis = jnp.concatenate([jnp.zeros((16, SUB)), basis, jnp.zeros((96, SUB))], axis=0).T

    def fill(first, ones_at, rest):
        out = jnp.where(lane == first, high, rest)
        out = jnp.where(lane == first + 1, mid, out)
        out = jnp.where(lane == first + 2, low, out)
        return jnp.where((lane >= ones_at) & (lane < ones_at + 3), 1.0, out)

    row_form, col_form = fill(4, 7, tail), fill(7, 4, tail + basis)
    is_first = lax.axis_index("core") == 0
    moved = jnp.where(is_first, row_form, col_form).astype(jnp.bfloat16)
    return moved, jnp.where(is_first, col_form, row_form).astype(jnp.bfloat16)


def prepare(coords_hbm, basis_hbm, out_ref, coords_ref, basis_ref, sems):
    copies = [
        pltpu.make_async_copy(coords_hbm, coords_ref, sems.at[0]),
        pltpu.make_async_copy(basis_hbm, basis_ref, sems.at[1]),
    ]
    for c in copies:
        c.start()
    for c in copies:
        c.wait()
    out_ref[:SUB, :896] = coords_ref[:, :896]
    out_ref[SUB:, :896] = coords_ref[:, :896]
    out_ref[:SUB, 896:], out_ref[SUB:, 896:] = forms(coords_ref, basis_ref)


def prepare_other(own_ref, coords_ref, basis_ref, base_ref, swapped_ref):
    base_ref[:SUB], swapped_ref[SUB:] = own_ref[:SUB], own_ref[SUB:]
    base_ref[SUB:, :896] = coords_ref[:, :896]
    swapped_ref[:SUB, :896] = coords_ref[:, :896]
    base_ref[SUB:, 896:], swapped_ref[:SUB, 896:] = forms(coords_ref, basis_ref)


def block_of(chip, core):
    dz, dyl = CHIPS[chip]
    ylo = lax.rem(lax.axis_index("ylo") + dyl, 2)
    return (ylo * 4 + lax.rem(lax.axis_index("z") + dz, 4)) * 2 + core


def start_all(plan, sems):
    copies = [
        pltpu.make_async_copy(src[k].at[pl.ds(at, n)], dst.at[pl.ds(to, n)], sems.at[sem])
        for sem, (src, dst, (k, at, to, n)) in enumerate(plan)
    ]
    for c in copies:
        c.start()
    for c in copies:
        c.wait()


def block_sums(r, rows, c, cols, out, pairs_ref, dens_ref, first=False):
    core = lax.axis_index("core")
    width = N_COLS[c]
    lane = lax.broadcasted_iota(jnp.int32, (1, width), 1)
    limits = {}
    for pair in sorted({CHIPS[k][1] for k in ROWS[r]}):
        limit = jnp.zeros((1, width), jnp.float32)
        for k, (chip, of) in enumerate(PARTS[c]):
            here = (lane >= k * SUB) & (lane < (k + 1) * SUB)
            live = pairs_ref[block_of(3 * pair, core), block_of(chip, of)] > 0
            limit = jnp.where(here, jnp.where(live, 0.0, NEG), limit)
        limits[pair] = limit
    totals = []
    for at in range(0, width, WIDE):
        ns = slice(at, at + WIDE)
        total = jnp.zeros((8, WIDE), jnp.float32)
        for m in range(0, N_ROWS[r], CHUNK):
            gram = lax.dot_general(
                rows[m : m + CHUNK, :],
                cols[ns, :],
                (((1,), (1,)), ((), ())),
                preferred_element_type=jnp.float32,
            )
            for k in range(CHUNK // SUB):
                limit = limits[CHIPS[ROWS[r][m // SUB + k]][1]][:, ns]
                kern = jnp.minimum(gram[k * SUB : (k + 1) * SUB] * SCALE, limit)
                kern = jnp.exp2(kern)
                out[m + k * SUB : m + (k + 1) * SUB, ns] = kern.astype(jnp.bfloat16)
                total += jnp.sum(kern.reshape(SUB // 8, 8, WIDE), axis=0)
        totals.append(jnp.sum(total, axis=0, keepdims=True))
    totals = jnp.concatenate(totals, axis=1)
    for k, (chip, of) in enumerate(PARTS[c]):
        row = pl.ds(block_of(chip, of), 1)
        total = totals[:, k * SUB : (k + 1) * SUB]
        dens_ref[row, :] = total if first else total + dens_ref[row, :]


def basis_of(cols):
    return cols[:, 896:].astype(jnp.float32).T[16:32].astype(jnp.bfloat16)


def pieces(ref, n):
    return [ref.at[pl.ds(k, n)] for k in range(0, ref.shape[0], n)]


def first_tile(pairs_ref, *refs):
    moved, (base_swapped, swapped, k00, dens, basis, rows, cols, sems) = refs[:4], refs[4:]
    swapped = [base_swapped] + pieces(swapped, CHUNK)
    for is_first in (True, False):

        @pl.when((lax.axis_index("core") == 0) == is_first)
        def _(is_first=is_first):
            row_from, col_from = (moved, swapped) if is_first else (swapped, moved)
            plan = [(row_from, rows, c) for c in ROW_COPIES[0][0 if is_first else 1]]
            start_all(plan + [(col_from, cols, c) for c in COL_COPIES[0]], sems)

    dens[...] = jnp.zeros_like(dens)
    block_sums(0, rows, 0, cols, k00, pairs_ref, dens, first=True)
    basis[...] = basis_of(cols)


def second_tile(pairs_ref, *refs):
    moved, swapped, refs = refs[:3], pieces(refs[3], 256), refs[4:]
    rows0, cols0, old, k01, k10, k11, dens, basis, rows, cols, sems = refs
    for is_first in (True, False):

        @pl.when((lax.axis_index("core") == 0) == is_first)
        def _(is_first=is_first):
            row_from, col_from = (moved, swapped) if is_first else (swapped, moved)
            plan = [(row_from, rows, c) for c in ROW_COPIES[1][0 if is_first else 1]]
            start_all(plan + [(col_from, cols, c) for c in COL_COPIES[1]], sems)

    dens[...] = old[...]
    block_sums(0, rows0, 1, cols, k01, pairs_ref, dens, first=True)
    block_sums(1, rows, 0, cols0, k10, pairs_ref, dens)
    block_sums(1, rows, 1, cols, k11, pairs_ref, dens)
    basis[...] = basis_of(cols)


def third_tile(pairs_ref, *refs):
    moved, refs = refs[:3], refs[3:]
    rows0, rows1, cols0, cols1, old, k20, k21, k02, k12, dens, held, sems = refs
    dens[...] = old[...]

    @pl.when(lax.axis_index("core") == 0)
    def _():
        start_all([(moved, held, c) for c in ROW_COPIES[2][0]], sems)
        rows = held.at[pl.ds(0, CHUNK)]
        block_sums(2, rows, 0, cols0, k20, pairs_ref, dens)
        block_sums(2, rows, 1, cols1, k21, pairs_ref, dens)

    @pl.when(lax.axis_index("core") == 1)
    def _():
        start_all([(moved, held, c) for c in COL_COPIES[2]], sems)
        block_sums(0, rows0, 2, held, k02, pairs_ref, dens)
        block_sums(1, rows1, 2, held, k12, pairs_ref, dens)


def fourth_tile(pairs_ref, *refs):
    swapped, refs = pieces(refs[0], 256), refs[1:]
    rows0, rows1, cols0, cols1, held, old, p20, p21, p02, p12 = refs[:10]
    k20, k21, k02, k12, k22, dens, basis, new, copy_sems, sems = refs[10:]
    dens[...] = old[...]

    def keep(*blocks):
        copies = [pltpu.make_async_copy(a, b, copy_sems.at[k]) for k, (a, b) in enumerate(blocks)]
        for c in copies:
            c.start()
        return copies

    @pl.when(lax.axis_index("core") == 0)
    def _():
        copies = keep((p20, k20), (p21, k21))
        start_all([(swapped, new, c) for c in COL_COPIES[2]], sems)
        basis[...] = basis_of(new)
        block_sums(0, rows0, 2, new, k02, pairs_ref, dens)
        block_sums(1, rows1, 2, new, k12, pairs_ref, dens)
        block_sums(2, held.at[pl.ds(0, CHUNK)], 2, new, k22, pairs_ref, dens)
        for c in copies:
            c.wait()

    @pl.when(lax.axis_index("core") == 1)
    def _():
        copies = keep((p02, k02), (p12, k12))
        start_all([(swapped, new, c) for c in ROW_COPIES[2][1]], sems)
        rows = new.at[pl.ds(0, CHUNK)]
        basis[...] = basis_of(held)
        block_sums(2, rows, 0, cols0, k20, pairs_ref, dens)
        block_sums(2, rows, 1, cols1, k21, pairs_ref, dens)
        block_sums(2, rows, 2, held, k22, pairs_ref, dens)
        for c in copies:
            c.wait()


def tile_call(kernel, pairs, operands, blocks, others, scratch=()):
    units = sum(N_ROWS[r] * N_COLS[c] for r, c in blocks)
    result = pl.pallas_call(
        kernel,
        in_specs=[SMEM] + [VMEM] * len(operands),
        out_specs=[VMEM] * (len(blocks) + len(others)),
        out_shape=[jax.ShapeDtypeStruct((N_ROWS[r], N_COLS[c]), jnp.bfloat16) for r, c in blocks]
        + [jax.ShapeDtypeStruct(*o) for o in others],
        scratch_shapes=[*scratch, pltpu.SemaphoreType.DMA((8,))],
        compiler_params=params(12),
        cost_estimate=pl.CostEstimate(flops=units, bytes_accessed=units, transcendentals=0),
        name=kernel.__name__,
    )(pairs, *operands)
    return dict(zip(blocks, result)), *result[len(blocks) :]


def scale_kernel(keys, t0, t1, b0, b1, b2, *refs):
    kern, refs = dict(zip(keys, refs)), refs[len(keys) :]
    there_ref, density_ref, s0, s1, s2, inv = refs
    total = t0[...] + t1[...]
    inv[...] = total
    density_ref[...] = inv[pl.ds(block_of(0, lax.axis_index("core")), 1), :]
    inv[...] = 1.0 / total
    for part, basis, scaled in zip(PARTS, (b0, b1, b2), (s0, s1, s2)):
        inverse = jnp.concatenate([inv[pl.ds(block_of(*s), 1), :] for s in part], axis=1)
        first = lax.broadcasted_iota(jnp.int32, (16, inverse.shape[1]), 0) == 0
        scaled[:16, :] = (basis[...].astype(jnp.float32) * inverse).astype(jnp.bfloat16)
        scaled[16:, :] = jnp.where(first, inverse, 0.0).astype(jnp.bfloat16)
    row_sums(1, (s0, s1, s2), kern, there_ref)


def here_kernel(keys, s0, s1, s2, *refs):
    row_sums(0, (s0, s1, s2), dict(zip(keys, refs)), refs[len(keys)])


def row_sums(pair, scaled, kern, out_ref):
    places = [(r, k) for r in range(3) for k, c in enumerate(ROWS[r]) if CHIPS[c][1] == pair]
    both = sum(
        lax.dot_general(
            s[...],
            jnp.concatenate([kern[r, c][k * SUB : (k + 1) * SUB, :] for r, k in places]),
            (((1,), (1,)), ((), ())),
            preferred_element_type=jnp.float32,
        )
        for c, s in enumerate(scaled)
    )
    for n, (r, k) in enumerate(places):
        part = both[:24, n * SUB : (n + 1) * SUB]
        dx = CHIPS[ROWS[r][k]][0]
        out_ref[dx * 16 : (dx + 1) * 16] = part[:16]
        out_ref[64 + dx : 65 + dx] = part[16:17]


def finish(a_ref, b_ref, c_ref, d_ref, out_ref):
    total = a_ref[...] + b_ref[...] + c_ref[...] + d_ref[...]
    out_ref[...] = total[:16] / total[16:17]


def body(coords, basis, pairs):
    f32 = lambda *s: jax.ShapeDtypeStruct(s, jnp.float32)
    form = lambda *s: jax.ShapeDtypeStruct((CHUNK, LANES), jnp.bfloat16)
    own = pl.pallas_call(
        prepare,
        in_specs=[pl.BlockSpec(memory_space=pltpu.HBM)] * 2,
        out_specs=VMEM,
        out_shape=form(),
        scratch_shapes=[
            pltpu.VMEM((SUB, D), jnp.bfloat16),
            pltpu.VMEM((16, SUB), jnp.bfloat16),
            pltpu.SemaphoreType.DMA((2,)),
        ],
        compiler_params=params(8),
        name="prepare",
    )(coords, basis)
    base, base_swapped = pl.pallas_call(
        prepare_other,
        in_specs=[VMEM] * 3,
        out_specs=[VMEM] * 2,
        out_shape=[form(), form()],
        compiler_params=params(8),
        name="prepare_other",
    )(own, swap(coords), swap(basis))
    join = lambda *arrays: jnp.concatenate(arrays)
    sums = ((16, SUB), jnp.float32)
    basis_cols = [((16, n), jnp.bfloat16) for n in N_COLS]
    frames = lambda n: ((n, LANES), jnp.bfloat16)

    over = across(base)
    down = along(base, -1)
    up = along(base, 1)
    swapped = swap(join(up, down, over))
    a3 = across(up[128:])
    a2 = along(down[128:], -1)
    a1 = along(join(up[:128], over[:128]), 1)
    kern, dens, b0, rows0, cols0 = tile_call(
        first_tile,
        pairs,
        (base, up, down, over, base_swapped, swapped),
        ((0, 0),),
        (sums, basis_cols[0], frames(N_ROWS[0]), frames(N_COLS[0])),
    )
    a1, a2, a3, dens, over, down = together(a1, a2, a3, dens, over, down)
    swapped = swap(join(a1, a2, a3))
    z3 = across(join(down[256:], a2[128:]))
    z2 = along(over[:256], -1)
    z1 = along(join(a1[128:], a3[:128]), 1)
    more, dens, b1, rows1, cols1 = tile_call(
        second_tile,
        pairs,
        (a1, a2, a3, swapped, rows0, cols0, dens),
        ((0, 1), (1, 0), (1, 1)),
        (sums, basis_cols[1], frames(N_ROWS[1]), frames(N_COLS[1])),
    )
    kern.update(more)
    dens, z3, z2, z1 = together(dens, z3, z2, z1)
    swapped = swap(join(z1, z2, z3))
    blocks = ((2, 0), (2, 1), (0, 2), (1, 2))
    more, dens, held = tile_call(
        third_tile,
        pairs,
        (z1, z2, z3, rows0, rows1, cols0, cols1, dens),
        blocks,
        (sums, frames(N_COLS[2])),
    )
    more, dens, b2 = tile_call(
        fourth_tile,
        pairs,
        (swapped, rows0, rows1, cols0, cols1, held, dens, *[more[k] for k in blocks]),
        blocks + ((2, 2),),
        (sums, basis_cols[2]),
        [pltpu.VMEM((N_COLS[2], LANES), jnp.bfloat16), pltpu.SemaphoreType.DMA((2,))],
    )
    kern.update(more)

    t = dens + swap(dens)
    t = t + fetch(t, dict(COL_PAIR, core=1))
    t = t + fetch(t, dict(z=lambda z: 3 - z, core=1))
    keys = tuple(sorted(kern))
    blocks = [kern[k] for k in keys]
    there, density, *scaled = pl.pallas_call(
        functools.partial(scale_kernel, keys),
        in_specs=[VMEM] * 14,
        out_specs=[VMEM] * 5,
        out_shape=[f32(72, SUB), f32(1, SUB)]
        + [jax.ShapeDtypeStruct((32, n), jnp.bfloat16) for n in N_COLS],
        scratch_shapes=[pltpu.VMEM((16, SUB), jnp.float32)],
        compiler_params=params(12),
        name="scale",
    )(t, fetch(t, dict(z=lambda z: z ^ 1, core=1)), b0, b1, b2, *blocks)
    here = pl.pallas_call(
        functools.partial(here_kernel, keys),
        in_specs=[VMEM] * 12,
        out_specs=VMEM,
        out_shape=f32(72, SUB),
        compiler_params=params(12),
        name="here",
    )(*scaled, *blocks)

    total = here + fetch(there, ROW_PAIR)
    shard = lambda k: jnp.concatenate([total[16 * k : 16 * k + 16], total[64 + k : 65 + k]])
    diffused = pl.pallas_call(
        finish,
        in_specs=[VMEM] * 4,
        out_specs=VMEM,
        out_shape=f32(16, SUB),
        compiler_params=params(8),
        name="finish",
    )(
        shard(0),
        fetch(shard(2), dict(x=2)),
        fetch(shard(1), dict(x=-1)),
        fetch(shard(3), dict(x=1)),
    )
    return diffused, density.reshape(SUB)


def solution(mesh):
    physical = Mesh(mesh.devices.reshape(SIZES), AXES)
    return jax.shard_map(
        body,
        mesh=physical,
        in_specs=(P(AXES, None), P(None, AXES), P()),
        out_specs=(P(None, AXES), P(AXES)),
        check_vma=False,
    )
```
